32 devices in a mesh: groups: 2 (over x), vid: 8 (over z, y), tok: 2 (over core).
Axes of the slice: x: 2, y: 2, z: 4, core: 2. Of those that a mesh axis runs over, the one named last changes fastest.
Arguments:
- captions: bfloat16 [16, 128, 32, 128], P(('groups', 'vid')), parts along dimension 0, may hold values from -8 to 8
- caption_lengths: int32 [16, 128], P(('groups', 'vid')), parts along dimension 0, may hold values from 1 to 32
- video_bank: bfloat16 [192, 256, 128], P(('groups', 'vid'), 'tok'), parts along dimension 0, may hold values from -1.5 to 1.5
- owner_order: int32 [6], P('groups'), parts along dimension 0, may hold values from 0 to 7, as said below
Outputs:
- scores: float32 [192, 384], P(('groups', 'vid')), parts along dimension 0
The draws below stay inside these ranges and needn't reach their ends.
There are 2 independent parts, one for each index of `groups`. The reference program is written for one: setup_inputs(seed, part) draws one part's arguments, and reference() takes and returns one part's arrays. A program takes and returns all parts, laid end to end along the dimension named above; each array names one. Nothing has to cross between parts.
Inputs may be any that keep to these rules, and one draw needn't show every extreme that they name: `caption_lengths`: token slot j of a caption is real when j is less than its count. `owner_order`: 3 different block indices.
All inputs are finite; a program needn't handle non-finite values.
Results may differ from the reference program's by a relative error of at most 0.0003.
Values may be sent and summed in bfloat16 or wider, within the bound.
A program may use at most 64 MiB of HBM per device.

```python
import jax
import jax.numpy as jnp
from jax import lax

D = 128
LQ = 32
VTOK = 256
CAPB = 128
ROUNDS = 3
VIDEOS = 96
CAP_OWNERS = 8


def draw_captions(key, part):
    shape_full = (CAP_OWNERS, CAPB, LQ, D)
    values_out = jnp.clip(jax.random.normal(jax.random.fold_in(key, 12), shape_full, jnp.float32), -6.0, 6.0)
    return jnp.clip(values_out, -8.0, 8.0).astype(jnp.bfloat16)


def draw_video_bank(key, part):
    shape_full = (VIDEOS, VTOK, D)
    spread = 0.6 * D ** (-0.5)
    values_out = jnp.clip(jax.random.normal(jax.random.fold_in(key, 23), shape_full, jnp.float32) * spread, -6.0 * spread, 6.0 * spread)
    return jnp.clip(values_out, -1.5, 1.5).astype(jnp.bfloat16)


def draw_owner_order(key, part):
    shuffled = jax.random.permutation(jax.random.fold_in(key, 31), CAP_OWNERS)
    return shuffled[:ROUNDS].astype(jnp.int32)


def plant(result, key, low, high):
    extent = result.shape
    place = [jax.random.randint(jax.random.fold_in(key, axis), (), 0, extent[axis]) for axis in range(len(extent))]
    result = result.at[tuple(place)].set(low)
    longest = extent.index(max(extent))
    place[longest] = (place[longest] + 1) % extent[longest]
    return result.at[tuple(place)].set(high)


def setup_inputs(seed: int = 0, part: int = 0) -> dict:
    seeds = jax.random.split(jax.random.key(seed), 5)
    own_keys = jax.random.split(jax.random.fold_in(seeds[4], part), 5)
    captions = draw_captions(jax.random.fold_in(jax.random.fold_in(seeds[4], part), 71), part)
    caption_lengths = plant(jax.random.randint(own_keys[1], (CAP_OWNERS, CAPB), 1, LQ + 1), jax.random.fold_in(own_keys[1], 1), 1, LQ).astype(jnp.int32)
    video_bank = draw_video_bank(jax.random.fold_in(jax.random.fold_in(seeds[4], part), 71), part)
    owner_order = draw_owner_order(jax.random.fold_in(jax.random.fold_in(seeds[4], part), 71), part)
    return {"captions": captions, "caption_lengths": caption_lengths, "video_bank": video_bank, "owner_order": owner_order}


sharpness_factor = 5.0


def reference(captions, caption_lengths, video_bank, owner_order):
    bank_full = video_bank.astype(jnp.float32)
    results = []
    for round_index in range(ROUNDS):
        caption_rows = captions[owner_order[round_index]].astype(jnp.float32)
        counts = caption_lengths[owner_order[round_index]]
        query_rows = caption_rows.reshape(CAPB * LQ, D)

        def per_video(footage_key_matrix):
            raw_similarity = jnp.dot(query_rows, footage_key_matrix.T, precision=lax.Precision.HIGHEST) * sharpness_factor
            row_peak = jnp.max(raw_similarity, axis=1)
            row_accumulated = jnp.sum(jnp.exp(raw_similarity - row_peak[:, None]), axis=1)
            return (row_peak + jnp.log(row_accumulated)) / sharpness_factor

        smoothed_scores = lax.map(per_video, bank_full).reshape(VIDEOS, CAPB, LQ)
        slots = jnp.arange(LQ, dtype=jnp.int32)
        lengths_float = counts.astype(jnp.float32)
        weights = (slots[None, :] < counts[:, None]).astype(jnp.float32) / lengths_float[:, None]
        results.append(jnp.einsum("vcj,cj->vc", smoothed_scores, weights, precision=lax.Precision.HIGHEST))
    return jnp.concatenate(results, axis=1)
```

```python
import functools
import math

import jax
import jax.numpy as jnp
from jax import lax
from jax.experimental import pallas as pl
from jax.experimental.pallas import tpu as pltpu
from jax.sharding import PartitionSpec as P

sharpness_factor = 5.0
SCALE = sharpness_factor * math.log2(math.e)
UNSCALE = math.log(2.0) / sharpness_factor

CHUNK_ROWS = 256
SKEW = 2
BANK_LAG = 4
MESH = pl.DeviceIdType.MESH


def kernel(
    n, rounds, slots,
    caps_ref, counts_ref, bank_ref, owner_ref, out_ref,
    mine, in_left, in_right, out_left, out_right, query, bank, counts_all, soft, acc, acc_in,
    own_sem, bank_sem, pair_send, pair_recv, right_send, right_recv, left_send, left_recv,
    count_send, count_recv, bank_send, bank_recv, acc_send, acc_recv,
):
    me = lax.axis_index("vid")
    tok = lax.axis_index("tok")
    place = me // 2
    side = me % 2
    mate = me + 1 - 2 * side
    other = 1 - tok
    line = n // 2
    subs = mine.shape[1]
    rows = mine.shape[2]
    chunks = subs * rounds
    videos = bank.shape[1]
    half = videos // 2
    mate_id = {"vid": mate, "tok": tok}
    twin_id = {"vid": me, "tok": other}
    cross_id = {"vid": mate, "tok": other}
    right_id = {"vid": me + 2, "tok": tok}
    left_id = {"vid": me - 2, "tok": tok}

    def remote(src, dst, send, recv, device):
        return pltpu.make_async_remote_copy(
            src_ref=src, dst_ref=dst, send_sem=send, recv_sem=recv,
            device_id=device, device_id_type=MESH,
        )

    def block_rows(of_side, sub):
        quarter = of_side * 2 + tok
        return pl.ds(pl.multiple_of((quarter * subs + sub) * rows, rows), rows)

    def own_copy(sub):
        return pltpu.make_async_copy(
            caps_ref.at[block_rows(side, sub)], mine.at[side, sub], own_sem.at[sub]
        )

    def pair_copy(sub):
        return remote(
            caps_ref.at[block_rows(1 - side, sub)], mine.at[side, sub],
            pair_send.at[sub], pair_recv.at[sub], mate_id,
        )

    def pair_arrival(sub):
        return remote(
            mine.at[1 - side, sub], mine.at[1 - side, sub],
            pair_send.at[sub], pair_recv.at[sub], mate_id,
        )

    def part(i):
        return pl.ds(i * half, half)

    bank_own = pltpu.make_async_copy(bank_ref, bank.at[0, :, tok], bank_sem)
    bank_twin = remote(
        bank_ref, bank.at[0, :, tok], bank_send.at[0], bank_recv.at[0], twin_id
    )

    def bank_pair(i):
        return remote(
            bank_ref.at[part(i)], bank.at[1, part(i), tok],
            bank_send.at[1 + i], bank_recv.at[1 + i], mate_id,
        )

    def bank_relay(i):
        return remote(
            bank.at[1, part(i), tok], bank.at[1, part(i), tok],
            bank_send.at[3 + i], bank_recv.at[3 + i], twin_id,
        )

    def bank_relayed(i):
        return remote(
            bank.at[1, part(i), other], bank.at[1, part(i), other],
            bank_send.at[3 + i], bank_recv.at[3 + i], twin_id,
        )

    def right_copy(k):
        return remote(
            out_right.at[k], in_left.at[k], right_send.at[k], right_recv.at[k], right_id
        )

    def left_copy(k):
        return remote(
            out_left.at[k], in_right.at[k], left_send.at[k], left_recv.at[k], left_id
        )

    def count_copy(to):
        return remote(
            counts_all.at[me], counts_all.at[me], count_send.at[to], count_recv.at[me],
            {"vid": to, "tok": tok},
        )

    def count_arrival(source):
        return remote(
            counts_all.at[source], counts_all.at[source], count_send.at[source],
            count_recv.at[source], {"vid": source, "tok": tok},
        )

    barrier = pltpu.get_barrier_semaphore()

    def greet(j, _):
        to = lax.rem(me + j, n)
        pl.semaphore_signal(barrier, inc=1, device_id={"vid": to, "tok": tok}, device_id_type=MESH)
        return 0

    lax.fori_loop(1, n, greet, 0)
    for device in (twin_id, cross_id):
        pl.semaphore_signal(barrier, inc=1, device_id=device, device_id_type=MESH)
    for sub in range(subs):
        own_copy(sub).start()
    bank_own.start()
    counts_all[me] = counts_ref[...]
    acc[...] = jnp.zeros_like(acc)
    pl.semaphore_wait(barrier, n + 1)

    pair_copy(0).start()

    def push(j, _):
        count_copy(lax.rem(me + j, n)).start()
        return 0

    lax.fori_loop(1, n, push, 0)
    bank_twin.start()

    def owner_of(k):
        return owner_ref[lax.rem(k, rounds)]

    def candidate(k):
        sub = k // rounds
        owner_side = jnp.full((rows, mine.shape[3]), lax.rem(owner_of(k), 2), jnp.int32)
        return jnp.where(
            owner_side == 0,
            mine[0, sub].astype(jnp.float32),
            mine[1, sub].astype(jnp.float32),
        )

    def owner_place(k):
        return jnp.full((rows, mine.shape[3]), owner_of(k) // 2, jnp.int32)

    def pick(k, incoming):
        return jnp.where(
            owner_place(k) == place, candidate(k), incoming.astype(jnp.float32)
        ).astype(jnp.bfloat16)

    def score(k, slot):
        q = query[k]
        group = 2

        def body(step, _):
            base = step * group
            tokens = bank[slot, pl.ds(base, group)]
            tokens = tokens.reshape(group * tokens.shape[1] * tokens.shape[2], tokens.shape[3])
            s = lax.dot_general(
                tokens, q, (((1,), (1,)), ((), ())), preferred_element_type=jnp.float32
            )
            s = s.reshape(group, s.shape[0] // group, rows)
            for g in range(group):
                sv = s[g]
                peak = jnp.max(sv, axis=0, keepdims=True)
                total = jnp.sum(jnp.exp2((sv - peak) * SCALE), axis=0, keepdims=True)
                soft[pl.ds(base + g, 1), :] = peak + UNSCALE * jnp.log2(total)
            return 0

        lax.fori_loop(0, videos // group, body, 0, unroll=2)
        r = lax.rem(k, rounds)
        first = ((side * 2 + tok) * subs + k // rounds) * (rows // slots)
        width = acc.shape[3]
        row = lax.broadcasted_iota(jnp.int32, (rows, width), 0)
        column = lax.broadcasted_iota(jnp.int32, (rows, width), 1)
        counts = counts_all[owner_of(k)]
        keep = (column == first + row // slots) & (row % slots < counts)
        keep = jnp.where(keep, 1.0, 0.0).astype(jnp.bfloat16)
        values = soft[...]
        high = values.astype(jnp.bfloat16)
        low = (values - high.astype(jnp.float32)).astype(jnp.bfloat16)
        acc[slot, r] += jnp.dot(high, keep, preferred_element_type=jnp.float32) + jnp.dot(
            low, keep, preferred_element_type=jnp.float32
        )

    near = jnp.minimum(place, line - 1 - place)
    far = jnp.maximum(place, line - 1 - place)

    def step_body(step, _):
        first_use = step - SKEW * near
        sub_now = first_use // rounds

        @pl.when((first_use >= 0) & (first_use < chunks) & (lax.rem(first_use + rounds, rounds) == 0))
        def _():
            own_copy(sub_now).wait()
            pair_arrival(sub_now).wait_recv()

            @pl.when(sub_now + 1 < subs)
            def _():
                pair_copy(sub_now + 1).start()

            for i in range(2):
                @pl.when(sub_now == i)
                def _():
                    bank_pair(i).start()

        k_right = step - SKEW * place

        @pl.when((k_right >= 0) & (k_right < chunks))
        def _():
            @pl.when(place > 0)
            def _():
                right_copy(k_right).wait_recv()

            @pl.when(place < line - 1)
            def _():
                out_right[k_right] = pick(k_right, in_left[k_right])
                right_copy(k_right).start()

        k_left = step - SKEW * (line - 1 - place)

        @pl.when((k_left >= 0) & (k_left < chunks))
        def _():
            @pl.when(place < line - 1)
            def _():
                left_copy(k_left).wait_recv()

            @pl.when(place > 0)
            def _():
                out_left[k_left] = pick(k_left, in_right[k_left])
                left_copy(k_left).start()

        k = step - SKEW * far

        @pl.when(k == 0)
        def _():
            bank_own.wait()
            bank_twin.wait_recv()

            def arrive(j, _):
                count_arrival(lax.rem(me + j, n)).wait_recv()
                return 0

            lax.fori_loop(1, n, arrive, 0)

        for i in range(2):
            @pl.when(k == BANK_LAG - 2 + i)
            def _():
                bank_pair(i).wait_recv()
                bank_relay(i).start()

        @pl.when(k == BANK_LAG)
        def _():
            for i in range(2):
                bank_relayed(i).wait_recv()

        @pl.when((k >= 0) & (k < chunks))
        def _():
            travelled = jnp.where(
                owner_place(k) < place,
                in_left[k].astype(jnp.float32),
                in_right[k].astype(jnp.float32),
            )
            query[k] = pick(k, travelled)
            score(k, 0)

        k_late = k - BANK_LAG

        @pl.when((k_late >= 0) & (k_late < chunks))
        def _():
            score(k_late, 1)

        return 0

    lax.fori_loop(0, chunks + SKEW * (line - 1) + BANK_LAG, step_body, 0)

    sends = [
        remote(acc.at[0], acc_in.at[0], acc_send.at[0], acc_recv.at[0], twin_id),
        remote(acc.at[1], acc_in.at[1], acc_send.at[1], acc_recv.at[1], mate_id),
        remote(acc.at[1], acc_in.at[2], acc_send.at[2], acc_recv.at[2], cross_id),
    ]
    for send in sends:
        send.start()

    def sent(j, _):
        count_copy(lax.rem(me + j, n)).wait_send()
        return 0

    lax.fori_loop(1, n, sent, 0)
    for sub in range(subs):
        pair_copy(sub).wait_send()
    bank_twin.wait_send()
    for i in range(2):
        bank_pair(i).wait_send()
        bank_relay(i).wait_send()

    def drain(k, _):
        @pl.when(place < line - 1)
        def _():
            right_copy(k).wait_send()

        @pl.when(place > 0)
        def _():
            left_copy(k).wait_send()

        return 0

    lax.fori_loop(0, chunks, drain, 0)
    for send in sends:
        send.wait()
    width = acc.shape[3]
    for r in range(rounds):
        total = acc[0, r] + acc_in[0, r] + acc_in[1, r] + acc_in[2, r]
        counts = counts_all[owner_ref[r]].astype(jnp.float32)
        out_ref[:, r * width : (r + 1) * width] = total / counts


def per_device(captions, caption_lengths, video_bank, owner_order):
    n = lax.axis_size("vid")
    parts = 2 * lax.axis_size("tok")
    _, blocks, slots, depth = captions.shape
    videos, tokens, _ = video_bank.shape
    rounds = owner_order.shape[0]
    rows = CHUNK_ROWS
    subs = blocks * slots // parts // rows
    chunks = subs * rounds
    bf16, f32 = jnp.bfloat16, jnp.float32
    stream = pltpu.VMEM((chunks, rows, depth), bf16)
    dma = pltpu.SemaphoreType.DMA
    logits = rounds * (blocks * slots // parts) * 2 * videos * 2 * tokens
    return pl.pallas_call(
        functools.partial(kernel, n, rounds, slots),
        out_shape=jax.ShapeDtypeStruct((videos, rounds * blocks), f32),
        in_specs=[
            pl.BlockSpec(memory_space=pl.ANY),
            pl.BlockSpec(memory_space=pltpu.VMEM),
            pl.BlockSpec(memory_space=pl.ANY),
            pl.BlockSpec(memory_space=pltpu.SMEM),
        ],
        out_specs=pl.BlockSpec(memory_space=pltpu.VMEM),
        scratch_shapes=[
            pltpu.VMEM((2, subs, rows, depth), bf16),
            stream, stream, stream, stream, stream,
            pltpu.VMEM((2, videos, 2, tokens, depth), bf16),
            pltpu.VMEM((n, 1, blocks), jnp.int32),
            pltpu.VMEM((videos, rows), f32),
            pltpu.VMEM((2, rounds, videos, blocks), f32),
            pltpu.VMEM((3, rounds, videos, blocks), f32),
            dma((subs,)), dma, dma((subs,)), dma((subs,)),
            dma((chunks,)), dma((chunks,)), dma((chunks,)), dma((chunks,)),
            dma((n,)), dma((n,)), dma((5,)), dma((5,)), dma((3,)), dma((3,)),
        ],
        compiler_params=pltpu.CompilerParams(
            collective_id=0, has_side_effects=True, vmem_limit_bytes=40 * 1024 * 1024
        ),
        cost_estimate=pl.CostEstimate(
            flops=2 * depth * logits, bytes_accessed=8 * 1024 * 1024, transcendentals=logits
        ),
    )(captions.reshape(blocks * slots, depth), caption_lengths, video_bank, owner_order)


def solution(mesh):
    return jax.shard_map(
        per_device,
        mesh=mesh,
        in_specs=(
            P(("groups", "vid"), None, None, None),
            P(("groups", "vid"), None),
            P(("groups", "vid"), "tok", None),
            P("groups"),
        ),
        out_specs=P(("groups", "vid"), None),
        check_vma=False,
    )
```

```python
import functools
import math

import jax
import jax.numpy as jnp
from jax import lax
from jax.experimental import pallas as pl
from jax.experimental.pallas import tpu as pltpu
from jax.sharding import PartitionSpec as P

sharpness_factor = 5.0
SCALE = sharpness_factor * math.log2(math.e)
UNSCALE = math.log(2.0) / sharpness_factor

CHUNK_ROWS = 256
SKEW = 2
BANK_LAG = 4
MESH = pl.DeviceIdType.MESH


def kernel(
    n, rounds, slots,
    caps_ref, counts_ref, bank_ref, owner_ref, out_ref,
    mine, in_left, in_right, out_left, out_right, query, bank, counts_all, soft, acc, acc_in,
    own_sem, bank_sem, pair_send, pair_recv, right_send, right_recv, left_send, left_recv,
    count_send, count_recv, bank_send, bank_recv, acc_send, acc_recv,
):
    me = lax.axis_index("vid")
    tok = lax.axis_index("tok")
    place = me // 2
    side = me % 2
    mate = me + 1 - 2 * side
    other = 1 - tok
    line = n // 2
    subs = mine.shape[1]
    rows = mine.shape[2]
    chunks = subs * rounds
    videos = bank.shape[1]
    half = videos // 2
    mate_id = {"vid": mate, "tok": tok}
    twin_id = {"vid": me, "tok": other}
    cross_id = {"vid": mate, "tok": other}
    right_id = {"vid": me + 2, "tok": tok}
    left_id = {"vid": me - 2, "tok": tok}

    def remote(src, dst, send, recv, device):
        return pltpu.make_async_remote_copy(
            src_ref=src, dst_ref=dst, send_sem=send, recv_sem=recv,
            device_id=device, device_id_type=MESH,
        )

    def block_rows(of_side, sub):
        quarter = of_side * 2 + tok
        return pl.ds(pl.multiple_of((quarter * subs + sub) * rows, rows), rows)

    def own_copy(sub):
        return pltpu.make_async_copy(
            caps_ref.at[block_rows(side, sub)], mine.at[side, sub], own_sem.at[sub]
        )

    def pair_copy(sub):
        return remote(
            caps_ref.at[block_rows(1 - side, sub)], mine.at[side, sub],
            pair_send.at[sub], pair_recv.at[sub], mate_id,
        )

    def pair_arrival(sub):
        return remote(
            mine.at[1 - side, sub], mine.at[1 - side, sub],
            pair_send.at[sub], pair_recv.at[sub], mate_id,
        )

    def part(i):
        return pl.ds(i * half, half)

    bank_own = pltpu.make_async_copy(bank_ref, bank.at[0, :, tok], bank_sem)
    bank_twin = remote(
        bank_ref, bank.at[0, :, tok], bank_send.at[0], bank_recv.at[0], twin_id
    )

    def bank_pair(i):
        return remote(
            bank_ref.at[part(i)], bank.at[1, part(i), tok],
            bank_send.at[1 + i], bank_recv.at[1 + i], mate_id,
        )

    def bank_relay(i):
        return remote(
            bank.at[1, part(i), tok], bank.at[1, part(i), tok],
            bank_send.at[3 + i], bank_recv.at[3 + i], twin_id,
        )

    def bank_relayed(i):
        return remote(
            bank.at[1, part(i), other], bank.at[1, part(i), other],
            bank_send.at[3 + i], bank_recv.at[3 + i], twin_id,
        )

    def right_copy(k):
        return remote(
            out_right.at[k], in_left.at[k], right_send.at[k], right_recv.at[k], right_id
        )

    def left_copy(k):
        return remote(
            out_left.at[k], in_right.at[k], left_send.at[k], left_recv.at[k], left_id
        )

    def count_copy(to):
        return remote(
            counts_all.at[me], counts_all.at[me], count_send.at[to], count_recv.at[me],
            {"vid": to, "tok": tok},
        )

    def count_arrival(source):
        return remote(
            counts_all.at[source], counts_all.at[source], count_send.at[source],
            count_recv.at[source], {"vid": source, "tok": tok},
        )

    barrier = pltpu.get_barrier_semaphore()

    def greet(j, _):
        to = lax.rem(me + j, n)
        pl.semaphore_signal(barrier, inc=1, device_id={"vid": to, "tok": tok}, device_id_type=MESH)
        return 0

    lax.fori_loop(1, n, greet, 0)
    for device in (twin_id, cross_id):
        pl.semaphore_signal(barrier, inc=1, device_id=device, device_id_type=MESH)
    for sub in range(subs):
        own_copy(sub).start()
    bank_own.start()
    counts_all[me] = counts_ref[...]
    acc[...] = jnp.zeros_like(acc)
    pl.semaphore_wait(barrier, n + 1)

    pair_copy(0).start()

    def push(j, _):
        count_copy(lax.rem(me + j, n)).start()
        return 0

    lax.fori_loop(1, n, push, 0)
    bank_twin.start()

    def owner_of(k):
        return owner_ref[lax.rem(k, rounds)]

    def candidate(k):
        sub = k // rounds
        owner_side = jnp.full((rows, mine.shape[3]), lax.rem(owner_of(k), 2), jnp.int32)
        return jnp.where(
            owner_side == 0,
            mine[0, sub].astype(jnp.float32),
            mine[1, sub].astype(jnp.float32),
        )

    def owner_place(k):
        return jnp.full((rows, mine.shape[3]), owner_of(k) // 2, jnp.int32)

    def pick(k, incoming):
        return jnp.where(
            owner_place(k) == place, candidate(k), incoming.astype(jnp.float32)
        ).astype(jnp.bfloat16)

    def score(k, slot):
        q = query[k].T

        def similarity(v):
            tokens = bank[slot, v].reshape(bank.shape[2] * bank.shape[3], bank.shape[4])
            return jnp.dot(tokens, q, preferred_element_type=jnp.float32)

        ahead = similarity(0)
        for v in range(videos):
            now = ahead
            if v + 1 < videos:
                ahead = similarity(v + 1)
            peak = jnp.max(now, axis=0, keepdims=True)
            total = jnp.sum(jnp.exp2((now - peak) * SCALE), axis=0, keepdims=True)
            soft[v : v + 1, :] = peak + UNSCALE * jnp.log2(total)
        r = lax.rem(k, rounds)
        first = ((side * 2 + tok) * subs + k // rounds) * (rows // slots)
        width = acc.shape[3]
        row = lax.broadcasted_iota(jnp.int32, (rows, width), 0)
        column = lax.broadcasted_iota(jnp.int32, (rows, width), 1)
        counts = counts_all[owner_of(k)]
        keep = (column == first + row // slots) & (row % slots < counts)
        keep = jnp.where(keep, 1.0, 0.0).astype(jnp.bfloat16)
        values = soft[...]
        high = values.astype(jnp.bfloat16)
        low = (values - high.astype(jnp.float32)).astype(jnp.bfloat16)
        acc[slot, r] += jnp.dot(high, keep, preferred_element_type=jnp.float32) + jnp.dot(
            low, keep, preferred_element_type=jnp.float32
        )

    near = jnp.minimum(place, line - 1 - place)
    far = jnp.maximum(place, line - 1 - place)

    def step_body(step, _):
        first_use = step - SKEW * near
        sub_now = first_use // rounds

        @pl.when((first_use >= 0) & (first_use < chunks) & (lax.rem(first_use + rounds, rounds) == 0))
        def _():
            own_copy(sub_now).wait()
            pair_arrival(sub_now).wait_recv()

            @pl.when(sub_now + 1 < subs)
            def _():
                pair_copy(sub_now + 1).start()

            for i in range(2):
                @pl.when(sub_now == i)
                def _():
                    bank_pair(i).start()

        k_right = step - SKEW * place

        @pl.when((k_right >= 0) & (k_right < chunks))
        def _():
            @pl.when(place > 0)
            def _():
                right_copy(k_right).wait_recv()

            @pl.when(place < line - 1)
            def _():
                out_right[k_right] = pick(k_right, in_left[k_right])
                right_copy(k_right).start()

        k_left = step - SKEW * (line - 1 - place)

        @pl.when((k_left >= 0) & (k_left < chunks))
        def _():
            @pl.when(place < line - 1)
            def _():
                left_copy(k_left).wait_recv()

            @pl.when(place > 0)
            def _():
                out_left[k_left] = pick(k_left, in_right[k_left])
                left_copy(k_left).start()

        k = step - SKEW * far

        @pl.when(k == 0)
        def _():
            bank_own.wait()
            bank_twin.wait_recv()

            def arrive(j, _):
                count_arrival(lax.rem(me + j, n)).wait_recv()
                return 0

            lax.fori_loop(1, n, arrive, 0)

        for i in range(2):
            @pl.when(k == BANK_LAG - 2 + i)
            def _():
                bank_pair(i).wait_recv()
                bank_relay(i).start()

        @pl.when(k == BANK_LAG)
        def _():
            for i in range(2):
                bank_relayed(i).wait_recv()

        @pl.when((k >= 0) & (k < chunks))
        def _():
            travelled = jnp.where(
                owner_place(k) < place,
                in_left[k].astype(jnp.float32),
                in_right[k].astype(jnp.float32),
            )
            query[k] = pick(k, travelled)
            score(k, 0)

        k_late = k - BANK_LAG

        @pl.when((k_late >= 0) & (k_late < chunks))
        def _():
            score(k_late, 1)

        return 0

    lax.fori_loop(0, chunks + SKEW * (line - 1) + BANK_LAG, step_body, 0)

    sends = [
        remote(acc.at[0], acc_in.at[0], acc_send.at[0], acc_recv.at[0], twin_id),
        remote(acc.at[1], acc_in.at[1], acc_send.at[1], acc_recv.at[1], mate_id),
        remote(acc.at[1], acc_in.at[2], acc_send.at[2], acc_recv.at[2], cross_id),
    ]
    for send in sends:
        send.start()

    def sent(j, _):
        count_copy(lax.rem(me + j, n)).wait_send()
        return 0

    lax.fori_loop(1, n, sent, 0)
    for sub in range(subs):
        pair_copy(sub).wait_send()
    bank_twin.wait_send()
    for i in range(2):
        bank_pair(i).wait_send()
        bank_relay(i).wait_send()

    def drain(k, _):
        @pl.when(place < line - 1)
        def _():
            right_copy(k).wait_send()

        @pl.when(place > 0)
        def _():
            left_copy(k).wait_send()

        return 0

    lax.fori_loop(0, chunks, drain, 0)
    for send in sends:
        send.wait()
    width = acc.shape[3]
    for r in range(rounds):
        total = acc[0, r] + acc_in[0, r] + acc_in[1, r] + acc_in[2, r]
        counts = counts_all[owner_ref[r]].astype(jnp.float32)
        out_ref[:, r * width : (r + 1) * width] = total / counts


def per_device(captions, caption_lengths, video_bank, owner_order):
    n = lax.axis_size("vid")
    parts = 2 * lax.axis_size("tok")
    _, blocks, slots, depth = captions.shape
    videos, tokens, _ = video_bank.shape
    rounds = owner_order.shape[0]
    rows = CHUNK_ROWS
    subs = blocks * slots // parts // rows
    chunks = subs * rounds
    bf16, f32 = jnp.bfloat16, jnp.float32
    stream = pltpu.VMEM((chunks, rows, depth), bf16)
    dma = pltpu.SemaphoreType.DMA
    logits = rounds * (blocks * slots // parts) * 2 * videos * 2 * tokens
    return pl.pallas_call(
        functools.partial(kernel, n, rounds, slots),
        out_shape=jax.ShapeDtypeStruct((videos, rounds * blocks), f32),
        in_specs=[
            pl.BlockSpec(memory_space=pltpu.HBM),
            pl.BlockSpec(memory_space=pltpu.VMEM),
            pl.BlockSpec(memory_space=pltpu.HBM),
            pl.BlockSpec(memory_space=pltpu.SMEM),
        ],
        out_specs=pl.BlockSpec(memory_space=pltpu.VMEM),
        scratch_shapes=[
            pltpu.VMEM((2, subs, rows, depth), bf16),
            stream, stream, stream, stream, stream,
            pltpu.VMEM((2, videos, 2, tokens, depth), bf16),
            pltpu.VMEM((n, 1, blocks), jnp.int32),
            pltpu.VMEM((videos, rows), f32),
            pltpu.VMEM((2, rounds, videos, blocks), f32),
            pltpu.VMEM((3, rounds, videos, blocks), f32),
            dma((subs,)), dma, dma((subs,)), dma((subs,)),
            dma((chunks,)), dma((chunks,)), dma((chunks,)), dma((chunks,)),
            dma((n,)), dma((n,)), dma((5,)), dma((5,)), dma((3,)), dma((3,)),
        ],
        compiler_params=pltpu.CompilerParams(
            collective_id=0, has_side_effects=True, vmem_limit_bytes=40 * 1024 * 1024
        ),
        cost_estimate=pl.CostEstimate(
            flops=2 * depth * logits, bytes_accessed=8 * 1024 * 1024, transcendentals=logits
        ),
    )(captions.reshape(blocks * slots, depth), caption_lengths, video_bank, owner_order)


def solution(mesh):
    return jax.shard_map(
        per_device,
        mesh=mesh,
        in_specs=(
            P(("groups", "vid"), None, None, None),
            P(("groups", "vid"), None),
            P(("groups", "vid"), "tok", None),
            P("groups"),
        ),
        out_specs=P(("groups", "vid"), None),
        check_vma=False,
    )
```

```python
import functools
import math

import jax
import jax.numpy as jnp
from jax import lax
from jax.experimental import pallas as pl
from jax.experimental.pallas import tpu as pltpu
from jax.sharding import PartitionSpec as P

sharpness_factor = 5.0
SCALE = sharpness_factor * math.log2(math.e)
UNSCALE = math.log(2.0) / sharpness_factor

CHUNK_ROWS = 256
SKEW = 2
BANK_LAG = 4
MESH = pl.DeviceIdType.MESH


def kernel(
    n, rounds, slots,
    caps_ref, counts_ref, bank_ref, owner_ref, out_ref,
    mine, in_left, in_right, out_left, out_right, query, bank, counts_all, peaks, sums, soft, acc, acc_in,
    own_sem, bank_sem, pair_send, pair_recv, right_send, right_recv, left_send, left_recv,
    count_send, count_recv, bank_send, bank_recv, acc_send, acc_recv,
):
    me = lax.axis_index("vid")
    tok = lax.axis_index("tok")
    place = me // 2
    side = me % 2
    mate = me + 1 - 2 * side
    other = 1 - tok
    line = n // 2
    subs = mine.shape[1]
    rows = mine.shape[2]
    chunks = subs * rounds
    videos = bank.shape[1]
    half = videos // 2
    mate_id = {"vid": mate, "tok": tok}
    twin_id = {"vid": me, "tok": other}
    cross_id = {"vid": mate, "tok": other}
    right_id = {"vid": me + 2, "tok": tok}
    left_id = {"vid": me - 2, "tok": tok}

    def remote(src, dst, send, recv, device):
        return pltpu.make_async_remote_copy(
            src_ref=src, dst_ref=dst, send_sem=send, recv_sem=recv,
            device_id=device, device_id_type=MESH,
        )

    def block_rows(of_side, sub):
        quarter = of_side * 2 + tok
        return pl.ds(pl.multiple_of((quarter * subs + sub) * rows, rows), rows)

    def own_copy(sub):
        return pltpu.make_async_copy(
            caps_ref.at[block_rows(side, sub)], mine.at[side, sub], own_sem.at[sub]
        )

    def pair_copy(sub):
        return remote(
            caps_ref.at[block_rows(1 - side, sub)], mine.at[side, sub],
            pair_send.at[sub], pair_recv.at[sub], mate_id,
        )

    def pair_arrival(sub):
        return remote(
            mine.at[1 - side, sub], mine.at[1 - side, sub],
            pair_send.at[sub], pair_recv.at[sub], mate_id,
        )

    def part(i):
        return pl.ds(i * half, half)

    bank_own = pltpu.make_async_copy(bank_ref, bank.at[0, :, tok], bank_sem)
    bank_twin = remote(
        bank_ref, bank.at[0, :, tok], bank_send.at[0], bank_recv.at[0], twin_id
    )

    def bank_pair(i):
        return remote(
            bank_ref.at[part(i)], bank.at[1, part(i), tok],
            bank_send.at[1 + i], bank_recv.at[1 + i], mate_id,
        )

    def bank_relay(i):
        return remote(
            bank.at[1, part(i), tok], bank.at[1, part(i), tok],
            bank_send.at[3 + i], bank_recv.at[3 + i], twin_id,
        )

    def bank_relayed(i):
        return remote(
            bank.at[1, part(i), other], bank.at[1, part(i), other],
            bank_send.at[3 + i], bank_recv.at[3 + i], twin_id,
        )

    def right_copy(k):
        return remote(
            out_right.at[k], in_left.at[k], right_send.at[k], right_recv.at[k], right_id
        )

    def left_copy(k):
        return remote(
            out_left.at[k], in_right.at[k], left_send.at[k], left_recv.at[k], left_id
        )

    def count_copy(to):
        return remote(
            counts_all.at[me], counts_all.at[me], count_send.at[to], count_recv.at[me],
            {"vid": to, "tok": tok},
        )

    def count_arrival(source):
        return remote(
            counts_all.at[source], counts_all.at[source], count_send.at[source],
            count_recv.at[source], {"vid": source, "tok": tok},
        )

    barrier = pltpu.get_barrier_semaphore()

    def greet(j, _):
        to = lax.rem(me + j, n)
        pl.semaphore_signal(barrier, inc=1, device_id={"vid": to, "tok": tok}, device_id_type=MESH)
        return 0

    lax.fori_loop(1, n, greet, 0)
    for device in (twin_id, cross_id):
        pl.semaphore_signal(barrier, inc=1, device_id=device, device_id_type=MESH)
    for sub in range(subs):
        own_copy(sub).start()
    bank_own.start()
    counts_all[me] = counts_ref[...]
    acc[...] = jnp.zeros_like(acc)
    pl.semaphore_wait(barrier, n + 1)

    pair_copy(0).start()

    def push(j, _):
        count_copy(lax.rem(me + j, n)).start()
        return 0

    lax.fori_loop(1, n, push, 0)
    bank_twin.start()

    def owner_of(k):
        return owner_ref[lax.rem(k, rounds)]

    def candidate(k):
        sub = k // rounds
        owner_side = jnp.full((rows, mine.shape[3]), lax.rem(owner_of(k), 2), jnp.int32)
        return jnp.where(
            owner_side == 0,
            mine[0, sub].astype(jnp.float32),
            mine[1, sub].astype(jnp.float32),
        )

    def owner_place(k):
        return jnp.full((rows, mine.shape[3]), owner_of(k) // 2, jnp.int32)

    def pick(k, incoming):
        return jnp.where(
            owner_place(k) == place, candidate(k), incoming.astype(jnp.float32)
        ).astype(jnp.bfloat16)

    def score(k, slot):
        q = query[k].T
        tiles = bank.shape[2]

        def similarity(b):
            return jnp.dot(
                bank[slot, b // tiles, b % tiles], q, preferred_element_type=jnp.float32
            )

        ahead = similarity(0)
        for b in range(videos * tiles):
            now = ahead.reshape(ahead.shape[0] // 8, 8, rows)
            if b + 1 < videos * tiles:
                ahead = similarity(b + 1)
            top = jnp.max(now, axis=0)
            peaks[b] = top
            sums[b] = jnp.sum(jnp.exp2((now - top[None]) * SCALE), axis=0)
        for v in range(videos):
            tops = peaks[v * tiles : (v + 1) * tiles].reshape(tiles * 8, rows)
            parts = sums[v * tiles : (v + 1) * tiles].reshape(tiles * 8, rows)
            peak = jnp.max(tops, axis=0, keepdims=True)
            total = jnp.sum(parts * jnp.exp2((tops - peak) * SCALE), axis=0, keepdims=True)
            soft[v : v + 1, :] = peak + UNSCALE * jnp.log2(total)
        r = lax.rem(k, rounds)
        first = ((side * 2 + tok) * subs + k // rounds) * (rows // slots)
        width = acc.shape[3]
        row = lax.broadcasted_iota(jnp.int32, (rows, width), 0)
        column = lax.broadcasted_iota(jnp.int32, (rows, width), 1)
        counts = counts_all[owner_of(k)]
        keep = (column == first + row // slots) & (row % slots < counts)
        keep = jnp.where(keep, 1.0, 0.0).astype(jnp.bfloat16)
        values = soft[...]
        high = values.astype(jnp.bfloat16)
        low = (values - high.astype(jnp.float32)).astype(jnp.bfloat16)
        acc[slot, r] += jnp.dot(high, keep, preferred_element_type=jnp.float32) + jnp.dot(
            low, keep, preferred_element_type=jnp.float32
        )

    near = jnp.minimum(place, line - 1 - place)
    far = jnp.maximum(place, line - 1 - place)

    def step_body(step, _):
        first_use = step - SKEW * near
        sub_now = first_use // rounds

        @pl.when((first_use >= 0) & (first_use < chunks) & (lax.rem(first_use + rounds, rounds) == 0))
        def _():
            own_copy(sub_now).wait()
            pair_arrival(sub_now).wait_recv()

            @pl.when(sub_now + 1 < subs)
            def _():
                pair_copy(sub_now + 1).start()

            for i in range(2):
                @pl.when(sub_now == i)
                def _():
                    bank_pair(i).start()

        k_right = step - SKEW * place

        @pl.when((k_right >= 0) & (k_right < chunks))
        def _():
            @pl.when(place > 0)
            def _():
                right_copy(k_right).wait_recv()

            @pl.when(place < line - 1)
            def _():
                out_right[k_right] = pick(k_right, in_left[k_right])
                right_copy(k_right).start()

        k_left = step - SKEW * (line - 1 - place)

        @pl.when((k_left >= 0) & (k_left < chunks))
        def _():
            @pl.when(place < line - 1)
            def _():
                left_copy(k_left).wait_recv()

            @pl.when(place > 0)
            def _():
                out_left[k_left] = pick(k_left, in_right[k_left])
                left_copy(k_left).start()

        k = step - SKEW * far

        @pl.when(k == 0)
        def _():
            bank_own.wait()
            bank_twin.wait_recv()

            def arrive(j, _):
                count_arrival(lax.rem(me + j, n)).wait_recv()
                return 0

            lax.fori_loop(1, n, arrive, 0)

        for i in range(2):
            @pl.when(k == BANK_LAG - 2 + i)
            def _():
                bank_pair(i).wait_recv()
                bank_relay(i).start()

        @pl.when(k == BANK_LAG)
        def _():
            for i in range(2):
                bank_relayed(i).wait_recv()

        @pl.when((k >= 0) & (k < chunks))
        def _():
            travelled = jnp.where(
                owner_place(k) < place,
                in_left[k].astype(jnp.float32),
                in_right[k].astype(jnp.float32),
            )
            query[k] = pick(k, travelled)
            score(k, 0)

        k_late = k - BANK_LAG

        @pl.when((k_late >= 0) & (k_late < chunks))
        def _():
            score(k_late, 1)

        return 0

    lax.fori_loop(0, chunks + SKEW * (line - 1) + BANK_LAG, step_body, 0)

    sends = [
        remote(acc.at[0], acc_in.at[0], acc_send.at[0], acc_recv.at[0], twin_id),
        remote(acc.at[1], acc_in.at[1], acc_send.at[1], acc_recv.at[1], mate_id),
        remote(acc.at[1], acc_in.at[2], acc_send.at[2], acc_recv.at[2], cross_id),
    ]
    for send in sends:
        send.start()

    def sent(j, _):
        count_copy(lax.rem(me + j, n)).wait_send()
        return 0

    lax.fori_loop(1, n, sent, 0)
    for sub in range(subs):
        pair_copy(sub).wait_send()
    bank_twin.wait_send()
    for i in range(2):
        bank_pair(i).wait_send()
        bank_relay(i).wait_send()

    def drain(k, _):
        @pl.when(place < line - 1)
        def _():
            right_copy(k).wait_send()

        @pl.when(place > 0)
        def _():
            left_copy(k).wait_send()

        return 0

    lax.fori_loop(0, chunks, drain, 0)
    for send in sends:
        send.wait()
    width = acc.shape[3]
    for r in range(rounds):
        total = acc[0, r] + acc_in[0, r] + acc_in[1, r] + acc_in[2, r]
        counts = counts_all[owner_ref[r]].astype(jnp.float32)
        out_ref[:, r * width : (r + 1) * width] = total / counts


def per_device(captions, caption_lengths, video_bank, owner_order):
    n = lax.axis_size("vid")
    parts = 2 * lax.axis_size("tok")
    _, blocks, slots, depth = captions.shape
    videos, tokens, _ = video_bank.shape
    rounds = owner_order.shape[0]
    rows = CHUNK_ROWS
    subs = blocks * slots // parts // rows
    chunks = subs * rounds
    bf16, f32 = jnp.bfloat16, jnp.float32
    stream = pltpu.VMEM((chunks, rows, depth), bf16)
    dma = pltpu.SemaphoreType.DMA
    logits = rounds * (blocks * slots // parts) * 2 * videos * 2 * tokens
    return pl.pallas_call(
        functools.partial(kernel, n, rounds, slots),
        out_shape=jax.ShapeDtypeStruct((videos, rounds * blocks), f32),
        in_specs=[
            pl.BlockSpec(memory_space=pltpu.HBM),
            pl.BlockSpec(memory_space=pltpu.VMEM),
            pl.BlockSpec(memory_space=pltpu.HBM),
            pl.BlockSpec(memory_space=pltpu.SMEM),
        ],
        out_specs=pl.BlockSpec(memory_space=pltpu.VMEM),
        scratch_shapes=[
            pltpu.VMEM((2, subs, rows, depth), bf16),
            stream, stream, stream, stream, stream,
            pltpu.VMEM((2, videos, 2, tokens, depth), bf16),
            pltpu.VMEM((n, 1, blocks), jnp.int32),
            pltpu.VMEM((2 * videos, 8, rows), f32),
            pltpu.VMEM((2 * videos, 8, rows), f32),
            pltpu.VMEM((videos, rows), f32),
            pltpu.VMEM((2, rounds, videos, blocks), f32),
            pltpu.VMEM((3, rounds, videos, blocks), f32),
            dma((subs,)), dma, dma((subs,)), dma((subs,)),
            dma((chunks,)), dma((chunks,)), dma((chunks,)), dma((chunks,)),
            dma((n,)), dma((n,)), dma((5,)), dma((5,)), dma((3,)), dma((3,)),
        ],
        compiler_params=pltpu.CompilerParams(
            collective_id=0, has_side_effects=True, vmem_limit_bytes=64 * 1024 * 1024 - 256 * 1024
        ),
        cost_estimate=pl.CostEstimate(
            flops=2 * depth * logits, bytes_accessed=8 * 1024 * 1024, transcendentals=logits
        ),
    )(captions.reshape(blocks * slots, depth), caption_lengths, video_bank, owner_order)


def solution(mesh):
    return jax.shard_map(
        per_device,
        mesh=mesh,
        in_specs=(
            P(("groups", "vid"), None, None, None),
            P(("groups", "vid"), None),
            P(("groups", "vid"), "tok", None),
            P("groups"),
        ),
        out_specs=P(("groups", "vid"), None),
        check_vma=False,
    )
```

```python
import functools
import math

import jax
import jax.numpy as jnp
from jax import lax
from jax.experimental import pallas as pl
from jax.experimental.pallas import tpu as pltpu
from jax.sharding import PartitionSpec as P

sharpness_factor = 5.0
SCALE = sharpness_factor * math.log2(math.e)
UNSCALE = math.log(2.0) / sharpness_factor

CHUNK_ROWS = 256
SKEW = 3
BANK_LAG = 4
MESH = pl.DeviceIdType.MESH


def kernel(
    n, rounds, slots,
    caps_ref, counts_ref, bank_ref, owner_ref, out_ref,
    mine, in_left, in_right, out_left, out_right, query, bank, counts_all, peaks, sums, soft, acc, acc_in,
    own_sem, bank_sem, pair_send, pair_recv, right_send, right_recv, left_send, left_recv,
    count_send, count_recv, bank_send, bank_recv, acc_send, acc_recv,
):
    me = lax.axis_index("vid")
    tok = lax.axis_index("tok")
    place = me // 2
    side = me % 2
    mate = me + 1 - 2 * side
    other = 1 - tok
    line = n // 2
    subs = mine.shape[1]
    rows = mine.shape[2]
    chunks = subs * rounds
    videos = bank.shape[1]
    half = videos // 2
    mate_id = {"vid": mate, "tok": tok}
    twin_id = {"vid": me, "tok": other}
    cross_id = {"vid": mate, "tok": other}
    right_id = {"vid": me + 2, "tok": tok}
    left_id = {"vid": me - 2, "tok": tok}

    def remote(src, dst, send, recv, device):
        return pltpu.make_async_remote_copy(
            src_ref=src, dst_ref=dst, send_sem=send, recv_sem=recv,
            device_id=device, device_id_type=MESH,
        )

    def block_rows(of_side, sub):
        quarter = of_side * 2 + tok
        return pl.ds(pl.multiple_of((quarter * subs + sub) * rows, rows), rows)

    def own_copy(sub):
        return pltpu.make_async_copy(
            caps_ref.at[block_rows(side, sub)], mine.at[side, sub], own_sem.at[sub]
        )

    def pair_copy(sub):
        return remote(
            caps_ref.at[block_rows(1 - side, sub)], mine.at[side, sub],
            pair_send.at[sub], pair_recv.at[sub], mate_id,
        )

    def pair_arrival(sub):
        return remote(
            mine.at[1 - side, sub], mine.at[1 - side, sub],
            pair_send.at[sub], pair_recv.at[sub], mate_id,
        )

    def part(i):
        return pl.ds(i * half, half)

    bank_own = pltpu.make_async_copy(bank_ref, bank.at[0, :, tok], bank_sem)
    bank_twin = remote(
        bank_ref, bank.at[0, :, tok], bank_send.at[0], bank_recv.at[0], twin_id
    )

    def bank_pair(i):
        return remote(
            bank_ref.at[part(i)], bank.at[1, part(i), tok],
            bank_send.at[1 + i], bank_recv.at[1 + i], mate_id,
        )

    def bank_relay(i):
        return remote(
            bank.at[1, part(i), tok], bank.at[1, part(i), tok],
            bank_send.at[3 + i], bank_recv.at[3 + i], twin_id,
        )

    def bank_relayed(i):
        return remote(
            bank.at[1, part(i), other], bank.at[1, part(i), other],
            bank_send.at[3 + i], bank_recv.at[3 + i], twin_id,
        )

    def right_copy(k):
        return remote(
            out_right.at[k], in_left.at[k], right_send.at[k], right_recv.at[k], right_id
        )

    def left_copy(k):
        return remote(
            out_left.at[k], in_right.at[k], left_send.at[k], left_recv.at[k], left_id
        )

    def count_copy(to):
        return remote(
            counts_all.at[me], counts_all.at[me], count_send.at[to], count_recv.at[me],
            {"vid": to, "tok": tok},
        )

    def count_arrival(source):
        return remote(
            counts_all.at[source], counts_all.at[source], count_send.at[source],
            count_recv.at[source], {"vid": source, "tok": tok},
        )

    barrier = pltpu.get_barrier_semaphore()

    def greet(j, _):
        to = lax.rem(me + j, n)
        pl.semaphore_signal(barrier, inc=1, device_id={"vid": to, "tok": tok}, device_id_type=MESH)
        return 0

    lax.fori_loop(1, n, greet, 0)
    for device in (twin_id, cross_id):
        pl.semaphore_signal(barrier, inc=1, device_id=device, device_id_type=MESH)
    for sub in range(subs):
        own_copy(sub).start()
    bank_own.start()
    counts_all[me] = counts_ref[...]
    acc[...] = jnp.zeros_like(acc)
    pl.semaphore_wait(barrier, n + 1)

    pair_copy(0).start()

    def push(j, _):
        count_copy(lax.rem(me + j, n)).start()
        return 0

    lax.fori_loop(1, n, push, 0)
    bank_twin.start()

    def owner_of(k):
        return owner_ref[lax.rem(k, rounds)]

    def candidate(k):
        sub = k // rounds
        owner_side = jnp.full((rows, mine.shape[3]), lax.rem(owner_of(k), 2), jnp.int32)
        return jnp.where(
            owner_side == 0,
            mine[0, sub].astype(jnp.float32),
            mine[1, sub].astype(jnp.float32),
        )

    def owner_place(k):
        return jnp.full((rows, mine.shape[3]), owner_of(k) // 2, jnp.int32)

    def pick(k, incoming):
        return jnp.where(
            owner_place(k) == place, candidate(k), incoming.astype(jnp.float32)
        ).astype(jnp.bfloat16)

    def score(k, slot):
        q = query[k].T
        tiles = bank.shape[2]

        group = math.gcd(videos, 4)

        def similarity(g):
            tokens = bank[slot, g * group : (g + 1) * group]
            tokens = tokens.reshape(group * tiles * bank.shape[3], bank.shape[4])
            s = jnp.dot(tokens, q, preferred_element_type=jnp.float32)
            return s.reshape(group * tiles, bank.shape[3] // 8, 8, rows)

        ahead = similarity(0)
        for g in range(videos // group):
            now = ahead
            if (g + 1) * group < videos:
                ahead = similarity(g + 1)
            for b in range(group * tiles):
                top = jnp.max(now[b], axis=0)
                peaks[g * group * tiles + b] = top
                sums[g * group * tiles + b] = jnp.sum(
                    jnp.exp2((now[b] - top[None]) * SCALE), axis=0
                )
        for v in range(videos):
            tops = peaks[v * tiles : (v + 1) * tiles].reshape(tiles * 8, rows)
            parts = sums[v * tiles : (v + 1) * tiles].reshape(tiles * 8, rows)
            peak = jnp.max(tops, axis=0, keepdims=True)
            total = jnp.sum(parts * jnp.exp2((tops - peak) * SCALE), axis=0, keepdims=True)
            soft[v : v + 1, :] = peak + UNSCALE * jnp.log2(total)
        r = lax.rem(k, rounds)
        first = ((side * 2 + tok) * subs + k // rounds) * (rows // slots)
        width = acc.shape[3]
        row = lax.broadcasted_iota(jnp.int32, (rows, width), 0)
        column = lax.broadcasted_iota(jnp.int32, (rows, width), 1)
        counts = counts_all[owner_of(k)]
        keep = (column == first + row // slots) & (row % slots < counts)
        keep = jnp.where(keep, 1.0, 0.0).astype(jnp.bfloat16)
        values = soft[...]
        high = values.astype(jnp.bfloat16)
        low = (values - high.astype(jnp.float32)).astype(jnp.bfloat16)
        acc[slot, r] += jnp.dot(high, keep, preferred_element_type=jnp.float32) + jnp.dot(
            low, keep, preferred_element_type=jnp.float32
        )

    near = jnp.minimum(place, line - 1 - place)
    far = jnp.maximum(place, line - 1 - place)

    def step_body(step, _):
        first_use = step - SKEW * near
        sub_now = first_use // rounds

        @pl.when((first_use >= 0) & (first_use < chunks) & (lax.rem(first_use + rounds, rounds) == 0))
        def _():
            own_copy(sub_now).wait()
            pair_arrival(sub_now).wait_recv()

            @pl.when(sub_now + 1 < subs)
            def _():
                pair_copy(sub_now + 1).start()

            for i in range(2):
                @pl.when(sub_now == i)
                def _():
                    bank_pair(i).start()

        k_right = step - SKEW * place

        @pl.when((k_right >= 0) & (k_right < chunks))
        def _():
            @pl.when(place > 0)
            def _():
                right_copy(k_right).wait_recv()

            @pl.when(place < line - 1)
            def _():
                out_right[k_right] = pick(k_right, in_left[k_right])
                right_copy(k_right).start()

        k_left = step - SKEW * (line - 1 - place)

        @pl.when((k_left >= 0) & (k_left < chunks))
        def _():
            @pl.when(place < line - 1)
            def _():
                left_copy(k_left).wait_recv()

            @pl.when(place > 0)
            def _():
                out_left[k_left] = pick(k_left, in_right[k_left])
                left_copy(k_left).start()

        k = step - SKEW * far

        @pl.when(k == 0)
        def _():
            bank_own.wait()
            bank_twin.wait_recv()

            def arrive(j, _):
                count_arrival(lax.rem(me + j, n)).wait_recv()
                return 0

            lax.fori_loop(1, n, arrive, 0)

        for i in range(2):
            @pl.when(k == BANK_LAG - 2 + i)
            def _():
                bank_pair(i).wait_recv()
                bank_relay(i).start()

        @pl.when(k == BANK_LAG)
        def _():
            for i in range(2):
                bank_relayed(i).wait_recv()

        @pl.when((k >= 0) & (k < chunks))
        def _():
            travelled = jnp.where(
                owner_place(k) < place,
                in_left[k].astype(jnp.float32),
                in_right[k].astype(jnp.float32),
            )
            query[k] = pick(k, travelled)
            score(k, 0)

        k_late = k - BANK_LAG

        @pl.when((k_late >= 0) & (k_late < chunks))
        def _():
            score(k_late, 1)

        return 0

    lax.fori_loop(0, chunks + SKEW * (line - 1) + BANK_LAG, step_body, 0)

    sends = [
        remote(acc.at[0], acc_in.at[0], acc_send.at[0], acc_recv.at[0], twin_id),
        remote(acc.at[1], acc_in.at[1], acc_send.at[1], acc_recv.at[1], mate_id),
        remote(acc.at[1], acc_in.at[2], acc_send.at[2], acc_recv.at[2], cross_id),
    ]
    for send in sends:
        send.start()

    def sent(j, _):
        count_copy(lax.rem(me + j, n)).wait_send()
        return 0

    lax.fori_loop(1, n, sent, 0)
    for sub in range(subs):
        pair_copy(sub).wait_send()
    bank_twin.wait_send()
    for i in range(2):
        bank_pair(i).wait_send()
        bank_relay(i).wait_send()

    def drain(k, _):
        @pl.when(place < line - 1)
        def _():
            right_copy(k).wait_send()

        @pl.when(place > 0)
        def _():
            left_copy(k).wait_send()

        return 0

    lax.fori_loop(0, chunks, drain, 0)
    for send in sends:
        send.wait()
    width = acc.shape[3]
    for r in range(rounds):
        total = acc[0, r] + acc_in[0, r] + acc_in[1, r] + acc_in[2, r]
        counts = counts_all[owner_ref[r]].astype(jnp.float32)
        out_ref[:, r * width : (r + 1) * width] = total / counts


def per_device(captions, caption_lengths, video_bank, owner_order):
    n = lax.axis_size("vid")
    parts = 2 * lax.axis_size("tok")
    _, blocks, slots, depth = captions.shape
    videos, tokens, _ = video_bank.shape
    rounds = owner_order.shape[0]
    rows = CHUNK_ROWS
    subs = blocks * slots // parts // rows
    chunks = subs * rounds
    bf16, f32 = jnp.bfloat16, jnp.float32
    stream = pltpu.VMEM((chunks, rows, depth), bf16)
    dma = pltpu.SemaphoreType.DMA
    logits = rounds * (blocks * slots // parts) * 2 * videos * 2 * tokens
    return pl.pallas_call(
        functools.partial(kernel, n, rounds, slots),
        out_shape=jax.ShapeDtypeStruct((videos, rounds * blocks), f32),
        in_specs=[
            pl.BlockSpec(memory_space=pltpu.HBM),
            pl.BlockSpec(memory_space=pltpu.VMEM),
            pl.BlockSpec(memory_space=pltpu.HBM),
            pl.BlockSpec(memory_space=pltpu.SMEM),
        ],
        out_specs=pl.BlockSpec(memory_space=pltpu.VMEM),
        scratch_shapes=[
            pltpu.VMEM((2, subs, rows, depth), bf16),
            stream, stream, stream, stream, stream,
            pltpu.VMEM((2, videos, 2, tokens, depth), bf16),
            pltpu.VMEM((n, 1, blocks), jnp.int32),
            pltpu.VMEM((2 * videos, 8, rows), f32),
            pltpu.VMEM((2 * videos, 8, rows), f32),
            pltpu.VMEM((videos, rows), f32),
            pltpu.VMEM((2, rounds, videos, blocks), f32),
            pltpu.VMEM((3, rounds, videos, blocks), f32),
            dma((subs,)), dma, dma((subs,)), dma((subs,)),
            dma((chunks,)), dma((chunks,)), dma((chunks,)), dma((chunks,)),
            dma((n,)), dma((n,)), dma((5,)), dma((5,)), dma((3,)), dma((3,)),
        ],
        compiler_params=pltpu.CompilerParams(
            collective_id=0, has_side_effects=True, vmem_limit_bytes=64 * 1024 * 1024 - 256 * 1024
        ),
        cost_estimate=pl.CostEstimate(
            flops=2 * depth * logits, bytes_accessed=8 * 1024 * 1024, transcendentals=logits
        ),
    )(captions.reshape(blocks * slots, depth), caption_lengths, video_bank, owner_order)


def solution(mesh):
    return jax.shard_map(
        per_device,
        mesh=mesh,
        in_specs=(
            P(("groups", "vid"), None, None, None),
            P(("groups", "vid"), None),
            P(("groups", "vid"), "tok", None),
            P("groups"),
        ),
        out_specs=P(("groups", "vid"), None),
        check_vma=False,
    )
```

```python
import functools
import math

import jax
import jax.numpy as jnp
from jax import lax
from jax.experimental import pallas as pl
from jax.experimental.pallas import tpu as pltpu
from jax.sharding import PartitionSpec as P

sharpness_factor = 5.0
SCALE = sharpness_factor * math.log2(math.e)
UNSCALE = math.log(2.0) / sharpness_factor

CHUNK_ROWS = 256
SKEW = 3
BANK_LAG = 4
MESH = pl.DeviceIdType.MESH


def kernel(
    n, rounds, slots,
    caps_ref, counts_ref, bank_ref, owner_ref, out_ref,
    mine, in_left, in_right, out_left, out_right, query, bank, counts_all, peaks, sums, soft, acc, acc_in,
    own_sem, bank_sem, pair_send, pair_recv, right_send, right_recv, left_send, left_recv,
    count_send, count_recv, bank_send, bank_recv, acc_send, acc_recv,
):
    me = lax.axis_index("vid")
    tok = lax.axis_index("tok")
    place = me // 2
    side = me % 2
    mate = me + 1 - 2 * side
    other = 1 - tok
    line = n // 2
    subs = mine.shape[1]
    rows = mine.shape[2]
    chunks = subs * rounds
    videos = bank.shape[1]
    half = videos // 2
    mate_id = {"vid": mate, "tok": tok}
    twin_id = {"vid": me, "tok": other}
    cross_id = {"vid": mate, "tok": other}
    right_id = {"vid": me + 2, "tok": tok}
    left_id = {"vid": me - 2, "tok": tok}

    def remote(src, dst, send, recv, device):
        return pltpu.make_async_remote_copy(
            src_ref=src, dst_ref=dst, send_sem=send, recv_sem=recv,
            device_id=device, device_id_type=MESH,
        )

    def block_rows(of_side, sub):
        quarter = of_side * 2 + tok
        return pl.ds(pl.multiple_of((quarter * subs + sub) * rows, rows), rows)

    def own_copy(sub):
        return pltpu.make_async_copy(
            caps_ref.at[block_rows(side, sub)], mine.at[side, sub], own_sem.at[sub]
        )

    def pair_copy(sub):
        return remote(
            caps_ref.at[block_rows(1 - side, sub)], mine.at[side, sub],
            pair_send.at[sub], pair_recv.at[sub], mate_id,
        )

    def pair_arrival(sub):
        return remote(
            mine.at[1 - side, sub], mine.at[1 - side, sub],
            pair_send.at[sub], pair_recv.at[sub], mate_id,
        )

    def part(i):
        return pl.ds(i * half, half)

    bank_own = pltpu.make_async_copy(bank_ref, bank.at[0, :, tok], bank_sem)
    bank_twin = remote(
        bank_ref, bank.at[0, :, tok], bank_send.at[0], bank_recv.at[0], twin_id
    )

    def bank_pair(i):
        return remote(
            bank_ref.at[part(i)], bank.at[1, part(i), tok],
            bank_send.at[1 + i], bank_recv.at[1 + i], mate_id,
        )

    def bank_relay(i):
        return remote(
            bank.at[1, part(i), tok], bank.at[1, part(i), tok],
            bank_send.at[3 + i], bank_recv.at[3 + i], twin_id,
        )

    def bank_relayed(i):
        return remote(
            bank.at[1, part(i), other], bank.at[1, part(i), other],
            bank_send.at[3 + i], bank_recv.at[3 + i], twin_id,
        )

    def right_copy(k):
        return remote(
            out_right.at[k], in_left.at[k], right_send.at[k], right_recv.at[k], right_id
        )

    def left_copy(k):
        return remote(
            out_left.at[k], in_right.at[k], left_send.at[k], left_recv.at[k], left_id
        )

    def count_copy(to):
        return remote(
            counts_all.at[me], counts_all.at[me], count_send.at[to], count_recv.at[me],
            {"vid": to, "tok": tok},
        )

    def count_arrival(source):
        return remote(
            counts_all.at[source], counts_all.at[source], count_send.at[source],
            count_recv.at[source], {"vid": source, "tok": tok},
        )

    barrier = pltpu.get_barrier_semaphore()

    def greet(j, _):
        to = lax.rem(me + j, n)
        pl.semaphore_signal(barrier, inc=1, device_id={"vid": to, "tok": tok}, device_id_type=MESH)
        return 0

    lax.fori_loop(1, n, greet, 0)
    for device in (twin_id, cross_id):
        pl.semaphore_signal(barrier, inc=1, device_id=device, device_id_type=MESH)
    for sub in range(subs):
        own_copy(sub).start()
    bank_own.start()
    counts_all[me] = counts_ref[...]
    acc[...] = jnp.zeros_like(acc)
    pl.semaphore_wait(barrier, n + 1)

    pair_copy(0).start()

    def push(j, _):
        count_copy(lax.rem(me + j, n)).start()
        return 0

    lax.fori_loop(1, n, push, 0)
    bank_twin.start()

    def owner_of(k):
        return owner_ref[lax.rem(k, rounds)]

    def candidate(k):
        sub = k // rounds
        owner_side = jnp.full((rows, mine.shape[3]), lax.rem(owner_of(k), 2), jnp.int32)
        return jnp.where(
            owner_side == 0,
            mine[0, sub].astype(jnp.float32),
            mine[1, sub].astype(jnp.float32),
        )

    def owner_place(k):
        return jnp.full((rows, mine.shape[3]), owner_of(k) // 2, jnp.int32)

    def pick(k, incoming):
        return jnp.where(
            owner_place(k) == place, candidate(k), incoming.astype(jnp.float32)
        ).astype(jnp.bfloat16)

    def score(k, slot):
        q = query[k].T
        tiles = bank.shape[2]

        group = math.gcd(videos, 4)

        def similarity(g):
            tokens = bank[slot, g * group : (g + 1) * group]
            tokens = tokens.reshape(group * tiles * bank.shape[3], bank.shape[4])
            s = jnp.dot(tokens, q, preferred_element_type=jnp.float32)
            return s.reshape(group * tiles, bank.shape[3] // 8, 8, rows)

        ahead = similarity(0)
        for g in range(videos // group):
            now = ahead
            if (g + 1) * group < videos:
                ahead = similarity(g + 1)
            for b in range(group * tiles):
                top = jnp.max(now[b], axis=0)
                peaks[g * group * tiles + b] = top
                powers = jnp.exp2(((now[b] - top[None]) * SCALE).astype(jnp.bfloat16))
                sums[g * group * tiles + b] = jnp.sum(powers.astype(jnp.float32), axis=0)
        for v in range(videos):
            tops = peaks[v * tiles : (v + 1) * tiles].reshape(tiles * 8, rows)
            parts = sums[v * tiles : (v + 1) * tiles].reshape(tiles * 8, rows)
            peak = jnp.max(tops, axis=0, keepdims=True)
            total = jnp.sum(parts * jnp.exp2((tops - peak) * SCALE), axis=0, keepdims=True)
            soft[v : v + 1, :] = peak + UNSCALE * jnp.log2(total)
        r = lax.rem(k, rounds)
        first = ((side * 2 + tok) * subs + k // rounds) * (rows // slots)
        width = acc.shape[3]
        row = lax.broadcasted_iota(jnp.int32, (rows, width), 0)
        column = lax.broadcasted_iota(jnp.int32, (rows, width), 1)
        counts = counts_all[owner_of(k)]
        keep = (column == first + row // slots) & (row % slots < counts)
        keep = jnp.where(keep, 1.0, 0.0).astype(jnp.bfloat16)
        values = soft[...]
        high = values.astype(jnp.bfloat16)
        low = (values - high.astype(jnp.float32)).astype(jnp.bfloat16)
        acc[slot, r] += jnp.dot(high, keep, preferred_element_type=jnp.float32) + jnp.dot(
            low, keep, preferred_element_type=jnp.float32
        )

    near = jnp.minimum(place, line - 1 - place)
    far = jnp.maximum(place, line - 1 - place)

    def step_body(step, _):
        first_use = step - SKEW * near
        sub_now = first_use // rounds

        @pl.when((first_use >= 0) & (first_use < chunks) & (lax.rem(first_use + rounds, rounds) == 0))
        def _():
            own_copy(sub_now).wait()
            pair_arrival(sub_now).wait_recv()

            @pl.when(sub_now + 1 < subs)
            def _():
                pair_copy(sub_now + 1).start()

            for i in range(2):
                @pl.when(sub_now == i)
                def _():
                    bank_pair(i).start()

        k_right = step - SKEW * place

        @pl.when((k_right >= 0) & (k_right < chunks))
        def _():
            @pl.when(place > 0)
            def _():
                right_copy(k_right).wait_recv()

            @pl.when(place < line - 1)
            def _():
                out_right[k_right] = pick(k_right, in_left[k_right])
                right_copy(k_right).start()

        k_left = step - SKEW * (line - 1 - place)

        @pl.when((k_left >= 0) & (k_left < chunks))
        def _():
            @pl.when(place < line - 1)
            def _():
                left_copy(k_left).wait_recv()

            @pl.when(place > 0)
            def _():
                out_left[k_left] = pick(k_left, in_right[k_left])
                left_copy(k_left).start()

        k = step - SKEW * far

        @pl.when(k == 0)
        def _():
            bank_own.wait()
            bank_twin.wait_recv()

            def arrive(j, _):
                count_arrival(lax.rem(me + j, n)).wait_recv()
                return 0

            lax.fori_loop(1, n, arrive, 0)

        for i in range(2):
            @pl.when(k == BANK_LAG - 2 + i)
            def _():
                bank_pair(i).wait_recv()
                bank_relay(i).start()

        @pl.when(k == BANK_LAG)
        def _():
            for i in range(2):
                bank_relayed(i).wait_recv()

        @pl.when((k >= 0) & (k < chunks))
        def _():
            travelled = jnp.where(
                owner_place(k) < place,
                in_left[k].astype(jnp.float32),
                in_right[k].astype(jnp.float32),
            )
            query[k] = pick(k, travelled)
            score(k, 0)

        k_late = k - BANK_LAG

        @pl.when((k_late >= 0) & (k_late < chunks))
        def _():
            score(k_late, 1)

        return 0

    lax.fori_loop(0, chunks + SKEW * (line - 1) + BANK_LAG, step_body, 0)

    sends = [
        remote(acc.at[0], acc_in.at[0], acc_send.at[0], acc_recv.at[0], twin_id),
        remote(acc.at[1], acc_in.at[1], acc_send.at[1], acc_recv.at[1], mate_id),
        remote(acc.at[1], acc_in.at[2], acc_send.at[2], acc_recv.at[2], cross_id),
    ]
    for send in sends:
        send.start()

    def sent(j, _):
        count_copy(lax.rem(me + j, n)).wait_send()
        return 0

    lax.fori_loop(1, n, sent, 0)
    for sub in range(subs):
        pair_copy(sub).wait_send()
    bank_twin.wait_send()
    for i in range(2):
        bank_pair(i).wait_send()
        bank_relay(i).wait_send()

    def drain(k, _):
        @pl.when(place < line - 1)
        def _():
            right_copy(k).wait_send()

        @pl.when(place > 0)
        def _():
            left_copy(k).wait_send()

        return 0

    lax.fori_loop(0, chunks, drain, 0)
    for send in sends:
        send.wait()
    width = acc.shape[3]
    for r in range(rounds):
        total = acc[0, r] + acc_in[0, r] + acc_in[1, r] + acc_in[2, r]
        counts = counts_all[owner_ref[r]].astype(jnp.float32)
        out_ref[:, r * width : (r + 1) * width] = total / counts


def per_device(captions, caption_lengths, video_bank, owner_order):
    n = lax.axis_size("vid")
    parts = 2 * lax.axis_size("tok")
    _, blocks, slots, depth = captions.shape
    videos, tokens, _ = video_bank.shape
    rounds = owner_order.shape[0]
    rows = CHUNK_ROWS
    subs = blocks * slots // parts // rows
    chunks = subs * rounds
    bf16, f32 = jnp.bfloat16, jnp.float32
    stream = pltpu.VMEM((chunks, rows, depth), bf16)
    dma = pltpu.SemaphoreType.DMA
    logits = rounds * (blocks * slots // parts) * 2 * videos * 2 * tokens
    return pl.pallas_call(
        functools.partial(kernel, n, rounds, slots),
        out_shape=jax.ShapeDtypeStruct((videos, rounds * blocks), f32),
        in_specs=[
            pl.BlockSpec(memory_space=pltpu.HBM),
            pl.BlockSpec(memory_space=pltpu.VMEM),
            pl.BlockSpec(memory_space=pltpu.HBM),
            pl.BlockSpec(memory_space=pltpu.SMEM),
        ],
        out_specs=pl.BlockSpec(memory_space=pltpu.VMEM),
        scratch_shapes=[
            pltpu.VMEM((2, subs, rows, depth), bf16),
            stream, stream, stream, stream, stream,
            pltpu.VMEM((2, videos, 2, tokens, depth), bf16),
            pltpu.VMEM((n, 1, blocks), jnp.int32),
            pltpu.VMEM((2 * videos, 8, rows), f32),
            pltpu.VMEM((2 * videos, 8, rows), f32),
            pltpu.VMEM((videos, rows), f32),
            pltpu.VMEM((2, rounds, videos, blocks), f32),
            pltpu.VMEM((3, rounds, videos, blocks), f32),
            dma((subs,)), dma, dma((subs,)), dma((subs,)),
            dma((chunks,)), dma((chunks,)), dma((chunks,)), dma((chunks,)),
            dma((n,)), dma((n,)), dma((5,)), dma((5,)), dma((3,)), dma((3,)),
        ],
        compiler_params=pltpu.CompilerParams(
            collective_id=0, has_side_effects=True, vmem_limit_bytes=64 * 1024 * 1024 - 256 * 1024
        ),
        cost_estimate=pl.CostEstimate(
            flops=2 * depth * logits, bytes_accessed=8 * 1024 * 1024, transcendentals=logits
        ),
    )(captions.reshape(blocks * slots, depth), caption_lengths, video_bank, owner_order)


def solution(mesh):
    return jax.shard_map(
        per_device,
        mesh=mesh,
        in_specs=(
            P(("groups", "vid"), None, None, None),
            P(("groups", "vid"), None),
            P(("groups", "vid"), "tok", None),
            P("groups"),
        ),
        out_specs=P(("groups", "vid"), None),
        check_vma=False,
    )
```

```python
import functools
import math

import jax
import jax.numpy as jnp
from jax import lax
from jax.experimental import pallas as pl
from jax.experimental.pallas import tpu as pltpu
from jax.sharding import PartitionSpec as P

sharpness_factor = 5.0
SCALE = sharpness_factor * math.log2(math.e)
UNSCALE = math.log(2.0) / sharpness_factor

CHUNK_ROWS = 256
SKEW = 3
BANK_LAG = 4
MESH = pl.DeviceIdType.MESH


def kernel(
    n, rounds, slots,
    caps_ref, counts_ref, bank_ref, owner_ref, out_ref,
    mine, in_left, in_right, out_left, out_right, query, bank, counts_all, peaks, sums, masks, acc, acc_in,
    own_sem, bank_sem, pair_send, pair_recv, right_send, right_recv, left_send, left_recv,
    count_send, count_recv, bank_send, bank_recv, acc_send, acc_recv,
):
    me = lax.axis_index("vid")
    tok = lax.axis_index("tok")
    place = me // 2
    side = me % 2
    mate = me + 1 - 2 * side
    other = 1 - tok
    line = n // 2
    subs = mine.shape[1]
    rows = mine.shape[2]
    chunks = subs * rounds
    videos = bank.shape[1]
    half = videos // 2
    mate_id = {"vid": mate, "tok": tok}
    twin_id = {"vid": me, "tok": other}
    cross_id = {"vid": mate, "tok": other}
    right_id = {"vid": me + 2, "tok": tok}
    left_id = {"vid": me - 2, "tok": tok}

    def remote(src, dst, send, recv, device):
        return pltpu.make_async_remote_copy(
            src_ref=src, dst_ref=dst, send_sem=send, recv_sem=recv,
            device_id=device, device_id_type=MESH,
        )

    def block_rows(of_side, sub):
        quarter = of_side * 2 + tok
        return pl.ds(pl.multiple_of((quarter * subs + sub) * rows, rows), rows)

    def own_copy(sub):
        return pltpu.make_async_copy(
            caps_ref.at[block_rows(side, sub)], mine.at[side, sub], own_sem.at[sub]
        )

    def pair_copy(sub):
        return remote(
            caps_ref.at[block_rows(1 - side, sub)], mine.at[side, sub],
            pair_send.at[sub], pair_recv.at[sub], mate_id,
        )

    def pair_arrival(sub):
        return remote(
            mine.at[1 - side, sub], mine.at[1 - side, sub],
            pair_send.at[sub], pair_recv.at[sub], mate_id,
        )

    def part(i):
        return pl.ds(i * half, half)

    bank_own = pltpu.make_async_copy(bank_ref, bank.at[0, :, tok], bank_sem)
    bank_twin = remote(
        bank_ref, bank.at[0, :, tok], bank_send.at[0], bank_recv.at[0], twin_id
    )

    def bank_pair(i):
        return remote(
            bank_ref.at[part(i)], bank.at[1, part(i), tok],
            bank_send.at[1 + i], bank_recv.at[1 + i], mate_id,
        )

    def bank_relay(i):
        return remote(
            bank.at[1, part(i), tok], bank.at[1, part(i), tok],
            bank_send.at[3 + i], bank_recv.at[3 + i], twin_id,
        )

    def bank_relayed(i):
        return remote(
            bank.at[1, part(i), other], bank.at[1, part(i), other],
            bank_send.at[3 + i], bank_recv.at[3 + i], twin_id,
        )

    def right_copy(k):
        return remote(
            out_right.at[k], in_left.at[k], right_send.at[k], right_recv.at[k], right_id
        )

    def left_copy(k):
        return remote(
            out_left.at[k], in_right.at[k], left_send.at[k], left_recv.at[k], left_id
        )

    def count_copy(to):
        return remote(
            counts_all.at[me], counts_all.at[me], count_send.at[to], count_recv.at[me],
            {"vid": to, "tok": tok},
        )

    def count_arrival(source):
        return remote(
            counts_all.at[source], counts_all.at[source], count_send.at[source],
            count_recv.at[source], {"vid": source, "tok": tok},
        )

    barrier = pltpu.get_barrier_semaphore()

    def greet(j, _):
        to = lax.rem(me + j, n)
        pl.semaphore_signal(barrier, inc=1, device_id={"vid": to, "tok": tok}, device_id_type=MESH)
        return 0

    lax.fori_loop(1, n, greet, 0)
    for device in (twin_id, cross_id):
        pl.semaphore_signal(barrier, inc=1, device_id=device, device_id_type=MESH)
    for sub in range(subs):
        own_copy(sub).start()
    bank_own.start()
    counts_all[me] = counts_ref[...]
    acc[...] = jnp.zeros_like(acc)
    pl.semaphore_wait(barrier, n + 1)

    pair_copy(0).start()

    def push(j, _):
        count_copy(lax.rem(me + j, n)).start()
        return 0

    lax.fori_loop(1, n, push, 0)
    bank_twin.start()

    def owner_of(k):
        return owner_ref[lax.rem(k, rounds)]

    def candidate(k):
        sub = k // rounds
        owner_side = jnp.full((rows, mine.shape[3]), lax.rem(owner_of(k), 2), jnp.int32)
        return jnp.where(
            owner_side == 0,
            mine[0, sub].astype(jnp.float32),
            mine[1, sub].astype(jnp.float32),
        )

    def owner_place(k):
        return jnp.full((rows, mine.shape[3]), owner_of(k) // 2, jnp.int32)

    def pick(k, incoming):
        return jnp.where(
            owner_place(k) == place, candidate(k), incoming.astype(jnp.float32)
        ).astype(jnp.bfloat16)

    def score(k, slot):
        q = query[k]
        tiles = bank.shape[2]

        group = math.gcd(videos, 4)

        def similarity(g):
            tokens = bank[slot, g * group : (g + 1) * group]
            tokens = tokens.reshape(group * tiles * bank.shape[3], bank.shape[4])
            s = jnp.dot(tokens, q, preferred_element_type=jnp.float32)
            return s.reshape(group, tiles * bank.shape[3] // 8, 8, rows)

        ahead = similarity(0)
        for g in range(videos // group):
            now = ahead
            if (g + 1) * group < videos:
                ahead = similarity(g + 1)
            for b in range(group):
                top = jnp.max(now[b], axis=0)
                peaks[g * group + b] = top
                sums[g * group + b] = jnp.sum(jnp.exp2((now[b] - top[None]) * SCALE), axis=0)
        tops = peaks[...]
        peak = jnp.max(tops, axis=1)
        weighed = sums[...] * jnp.exp2((tops - peak[:, None, :]) * SCALE)
        values = peak + UNSCALE * jnp.log2(jnp.sum(weighed, axis=1))
        r = lax.rem(k, rounds)
        keep = masks[k]
        high = values.astype(jnp.bfloat16)
        low = (values - high.astype(jnp.float32)).astype(jnp.bfloat16)
        acc[slot, r] += jnp.dot(high, keep, preferred_element_type=jnp.float32) + jnp.dot(
            low, keep, preferred_element_type=jnp.float32
        )

    def mask(k):
        first = ((side * 2 + tok) * subs + k // rounds) * (rows // slots)
        width = acc.shape[3]
        row = lax.broadcasted_iota(jnp.int32, (rows, width), 0)
        column = lax.broadcasted_iota(jnp.int32, (rows, width), 1)
        counts = counts_all[owner_of(k)]
        keep = (column == first + row // slots) & (row % slots < counts)
        return jnp.where(keep, 1.0, 0.0).astype(jnp.bfloat16)

    near = jnp.minimum(place, line - 1 - place)
    far = jnp.maximum(place, line - 1 - place)

    def step_body(step, _):
        first_use = step - SKEW * near
        sub_now = first_use // rounds

        @pl.when((first_use >= 0) & (first_use < chunks) & (lax.rem(first_use + rounds, rounds) == 0))
        def _():
            own_copy(sub_now).wait()
            pair_arrival(sub_now).wait_recv()

            @pl.when(sub_now + 1 < subs)
            def _():
                pair_copy(sub_now + 1).start()

            for i in range(2):
                @pl.when(sub_now == i)
                def _():
                    bank_pair(i).start()

        k_right = step - SKEW * place

        @pl.when((k_right >= 0) & (k_right < chunks))
        def _():
            @pl.when(place > 0)
            def _():
                right_copy(k_right).wait_recv()

            @pl.when(place < line - 1)
            def _():
                out_right[k_right] = pick(k_right, in_left[k_right])
                right_copy(k_right).start()

        k_left = step - SKEW * (line - 1 - place)

        @pl.when((k_left >= 0) & (k_left < chunks))
        def _():
            @pl.when(place < line - 1)
            def _():
                left_copy(k_left).wait_recv()

            @pl.when(place > 0)
            def _():
                out_left[k_left] = pick(k_left, in_right[k_left])
                left_copy(k_left).start()

        k = step - SKEW * far

        @pl.when(k == 0)
        def _():
            bank_own.wait()
            bank_twin.wait_recv()

            def arrive(j, _):
                count_arrival(lax.rem(me + j, n)).wait_recv()
                return 0

            lax.fori_loop(1, n, arrive, 0)

        for i in range(2):
            @pl.when(k == BANK_LAG - 2 + i)
            def _():
                bank_pair(i).wait_recv()
                bank_relay(i).start()

        @pl.when(k == BANK_LAG)
        def _():
            for i in range(2):
                bank_relayed(i).wait_recv()

        @pl.when((k >= 0) & (k < chunks))
        def _():
            travelled = jnp.where(
                owner_place(k) < place,
                in_left[k].astype(jnp.float32),
                in_right[k].astype(jnp.float32),
            )
            query[k] = pick(k, travelled).T
            masks[k] = mask(k)
            score(k, 0)

        k_late = k - BANK_LAG

        @pl.when((k_late >= 0) & (k_late < chunks))
        def _():
            score(k_late, 1)

        return 0

    lax.fori_loop(0, chunks + SKEW * (line - 1) + BANK_LAG, step_body, 0)

    sends = [
        remote(acc.at[0], acc_in.at[0], acc_send.at[0], acc_recv.at[0], twin_id),
        remote(acc.at[1], acc_in.at[1], acc_send.at[1], acc_recv.at[1], mate_id),
        remote(acc.at[1], acc_in.at[2], acc_send.at[2], acc_recv.at[2], cross_id),
    ]
    for send in sends:
        send.start()

    def sent(j, _):
        count_copy(lax.rem(me + j, n)).wait_send()
        return 0

    lax.fori_loop(1, n, sent, 0)
    for sub in range(subs):
        pair_copy(sub).wait_send()
    bank_twin.wait_send()
    for i in range(2):
        bank_pair(i).wait_send()
        bank_relay(i).wait_send()

    def drain(k, _):
        @pl.when(place < line - 1)
        def _():
            right_copy(k).wait_send()

        @pl.when(place > 0)
        def _():
            left_copy(k).wait_send()

        return 0

    lax.fori_loop(0, chunks, drain, 0)
    for send in sends:
        send.wait()
    width = acc.shape[3]
    for r in range(rounds):
        total = acc[0, r] + acc_in[0, r] + acc_in[1, r] + acc_in[2, r]
        counts = counts_all[owner_ref[r]].astype(jnp.float32)
        out_ref[:, r * width : (r + 1) * width] = total / counts


def per_device(captions, caption_lengths, video_bank, owner_order):
    n = lax.axis_size("vid")
    parts = 2 * lax.axis_size("tok")
    _, blocks, slots, depth = captions.shape
    videos, tokens, _ = video_bank.shape
    rounds = owner_order.shape[0]
    rows = CHUNK_ROWS
    subs = blocks * slots // parts // rows
    chunks = subs * rounds
    bf16, f32 = jnp.bfloat16, jnp.float32
    stream = pltpu.VMEM((chunks, rows, depth), bf16)
    dma = pltpu.SemaphoreType.DMA
    logits = rounds * (blocks * slots // parts) * 2 * videos * 2 * tokens
    return pl.pallas_call(
        functools.partial(kernel, n, rounds, slots),
        out_shape=jax.ShapeDtypeStruct((videos, rounds * blocks), f32),
        in_specs=[
            pl.BlockSpec(memory_space=pltpu.HBM),
            pl.BlockSpec(memory_space=pltpu.VMEM),
            pl.BlockSpec(memory_space=pltpu.HBM),
            pl.BlockSpec(memory_space=pltpu.SMEM),
        ],
        out_specs=pl.BlockSpec(memory_space=pltpu.VMEM),
        scratch_shapes=[
            pltpu.VMEM((2, subs, rows, depth), bf16),
            stream, stream, stream, stream,
            pltpu.VMEM((chunks, depth, rows), bf16),
            pltpu.VMEM((2, videos, 2, tokens, depth), bf16),
            pltpu.VMEM((n, 1, blocks), jnp.int32),
            pltpu.VMEM((videos, 8, rows), f32),
            pltpu.VMEM((videos, 8, rows), f32),
            pltpu.VMEM((chunks, rows, blocks), bf16),
            pltpu.VMEM((2, rounds, videos, blocks), f32),
            pltpu.VMEM((3, rounds, videos, blocks), f32),
            dma((subs,)), dma, dma((subs,)), dma((subs,)),
            dma((chunks,)), dma((chunks,)), dma((chunks,)), dma((chunks,)),
            dma((n,)), dma((n,)), dma((5,)), dma((5,)), dma((3,)), dma((3,)),
        ],
        compiler_params=pltpu.CompilerParams(
            collective_id=0, has_side_effects=True, vmem_limit_bytes=64 * 1024 * 1024 - 256 * 1024
        ),
        cost_estimate=pl.CostEstimate(
            flops=2 * depth * logits, bytes_accessed=8 * 1024 * 1024, transcendentals=logits
        ),
    )(captions.reshape(blocks * slots, depth), caption_lengths, video_bank, owner_order)


def solution(mesh):
    return jax.shard_map(
        per_device,
        mesh=mesh,
        in_specs=(
            P(("groups", "vid"), None, None, None),
            P(("groups", "vid"), None),
            P(("groups", "vid"), "tok", None),
            P("groups"),
        ),
        out_specs=P(("groups", "vid"), None),
        check_vma=False,
    )
```

```python
import functools
import math

import jax
import jax.numpy as jnp
from jax import lax
from jax.experimental import pallas as pl
from jax.experimental.pallas import tpu as pltpu
from jax.sharding import PartitionSpec as P

sharpness_factor = 5.0
SCALE = sharpness_factor * math.log2(math.e)
UNSCALE = math.log(2.0) / sharpness_factor

CHUNK_ROWS = 256
LANES = 128
SKEW = 3
BANK_LAG = 4
MESH = pl.DeviceIdType.MESH


def kernel(
    n, rounds, slots,
    caps_ref, counts_ref, bank_ref, owner_ref, out_ref,
    mine, in_left, in_right, out_left, out_right, query, bank, counts_all, peaks, sums, masks, acc, acc_in,
    own_sem, bank_sem, pair_send, pair_recv, right_send, right_recv, left_send, left_recv,
    count_send, count_recv, bank_send, bank_recv, acc_send, acc_recv,
):
    me = lax.axis_index("vid")
    tok = lax.axis_index("tok")
    place = me // 2
    side = me % 2
    mate = me + 1 - 2 * side
    other = 1 - tok
    line = n // 2
    subs = mine.shape[1]
    rows = mine.shape[2]
    chunks = subs * rounds
    videos = bank.shape[1]
    half = videos // 2
    mate_id = {"vid": mate, "tok": tok}
    twin_id = {"vid": me, "tok": other}
    cross_id = {"vid": mate, "tok": other}
    right_id = {"vid": me + 2, "tok": tok}
    left_id = {"vid": me - 2, "tok": tok}

    def remote(src, dst, send, recv, device):
        return pltpu.make_async_remote_copy(
            src_ref=src, dst_ref=dst, send_sem=send, recv_sem=recv,
            device_id=device, device_id_type=MESH,
        )

    def block_rows(of_side, sub):
        quarter = of_side * 2 + tok
        return pl.ds(pl.multiple_of((quarter * subs + sub) * rows, rows), rows)

    def own_copy(sub):
        return pltpu.make_async_copy(
            caps_ref.at[block_rows(side, sub)], mine.at[side, sub], own_sem.at[sub]
        )

    def pair_copy(sub):
        return remote(
            caps_ref.at[block_rows(1 - side, sub)], mine.at[side, sub],
            pair_send.at[sub], pair_recv.at[sub], mate_id,
        )

    def pair_arrival(sub):
        return remote(
            mine.at[1 - side, sub], mine.at[1 - side, sub],
            pair_send.at[sub], pair_recv.at[sub], mate_id,
        )

    def part(i):
        return pl.ds(i * half, half)

    bank_own = pltpu.make_async_copy(bank_ref, bank.at[0, :, tok], bank_sem)
    bank_twin = remote(
        bank_ref, bank.at[0, :, tok], bank_send.at[0], bank_recv.at[0], twin_id
    )

    def bank_pair(i):
        return remote(
            bank_ref.at[part(i)], bank.at[1, part(i), tok],
            bank_send.at[1 + i], bank_recv.at[1 + i], mate_id,
        )

    def bank_relay(i):
        return remote(
            bank.at[1, part(i), tok], bank.at[1, part(i), tok],
            bank_send.at[3 + i], bank_recv.at[3 + i], twin_id,
        )

    def bank_relayed(i):
        return remote(
            bank.at[1, part(i), other], bank.at[1, part(i), other],
            bank_send.at[3 + i], bank_recv.at[3 + i], twin_id,
        )

    def right_copy(k):
        return remote(
            out_right.at[k], in_left.at[k], right_send.at[k], right_recv.at[k], right_id
        )

    def left_copy(k):
        return remote(
            out_left.at[k], in_right.at[k], left_send.at[k], left_recv.at[k], left_id
        )

    def count_copy(to):
        return remote(
            counts_all.at[me], counts_all.at[me], count_send.at[to], count_recv.at[me],
            {"vid": to, "tok": tok},
        )

    def count_arrival(source):
        return remote(
            counts_all.at[source], counts_all.at[source], count_send.at[source],
            count_recv.at[source], {"vid": source, "tok": tok},
        )

    barrier = pltpu.get_barrier_semaphore()

    def greet(j, _):
        to = lax.rem(me + j, n)
        pl.semaphore_signal(barrier, inc=1, device_id={"vid": to, "tok": tok}, device_id_type=MESH)
        return 0

    lax.fori_loop(1, n, greet, 0)
    for device in (twin_id, cross_id):
        pl.semaphore_signal(barrier, inc=1, device_id=device, device_id_type=MESH)
    for sub in range(subs):
        own_copy(sub).start()
    bank_own.start()
    counts_all[me] = counts_ref[...]
    acc[...] = jnp.zeros_like(acc)
    pl.semaphore_wait(barrier, n + 1)

    pair_copy(0).start()

    def push(j, _):
        count_copy(lax.rem(me + j, n)).start()
        return 0

    lax.fori_loop(1, n, push, 0)
    bank_twin.start()

    def owner_of(k):
        return owner_ref[lax.rem(k, rounds)]

    def candidate(k):
        sub = k // rounds
        owner_side = jnp.full((rows, mine.shape[3]), lax.rem(owner_of(k), 2), jnp.int32)
        return jnp.where(
            owner_side == 0,
            mine[0, sub].astype(jnp.float32),
            mine[1, sub].astype(jnp.float32),
        )

    def owner_place(k):
        return jnp.full((rows, mine.shape[3]), owner_of(k) // 2, jnp.int32)

    def pick(k, incoming):
        return jnp.where(
            owner_place(k) == place, candidate(k), incoming.astype(jnp.float32)
        ).astype(jnp.bfloat16)

    def score(k, slot):
        q = query[k]
        tiles = bank.shape[2]

        group = math.gcd(videos, 4)

        def similarity(g):
            tokens = bank[slot, g * group : (g + 1) * group]
            tokens = tokens.reshape(group * tiles * bank.shape[3], bank.shape[4])
            s = jnp.dot(tokens, q, preferred_element_type=jnp.float32)
            return s.reshape(group * tiles, bank.shape[3] // 8, 8, rows)

        ahead = similarity(0)
        for g in range(videos // group):
            now = ahead
            if (g + 1) * group < videos:
                ahead = similarity(g + 1)
            for b in range(group * tiles):
                for lane in range(0, rows, LANES):
                    block = now[b, :, :, lane : lane + LANES]
                    top = jnp.max(block, axis=0)
                    powers = jnp.exp2((block - top[None]) * SCALE)
                    video, tile = divmod(g * group * tiles + b, tiles)
                    peaks[video, tile * 8 : tile * 8 + 8, lane : lane + LANES] = top
                    sums[video, tile * 8 : tile * 8 + 8, lane : lane + LANES] = jnp.sum(powers, axis=0)
        tops = peaks[...]
        peak = jnp.max(tops, axis=1)
        weighed = sums[...] * jnp.exp2((tops - peak[:, None, :]) * SCALE)
        values = peak + UNSCALE * jnp.log2(jnp.sum(weighed, axis=1))
        r = lax.rem(k, rounds)
        keep = masks[k]
        high = values.astype(jnp.bfloat16)
        low = (values - high.astype(jnp.float32)).astype(jnp.bfloat16)
        acc[slot, r] += jnp.dot(high, keep, preferred_element_type=jnp.float32) + jnp.dot(
            low, keep, preferred_element_type=jnp.float32
        )

    def mask(k):
        first = ((side * 2 + tok) * subs + k // rounds) * (rows // slots)
        width = acc.shape[3]
        row = lax.broadcasted_iota(jnp.int32, (rows, width), 0)
        column = lax.broadcasted_iota(jnp.int32, (rows, width), 1)
        counts = counts_all[owner_of(k)]
        keep = (column == first + row // slots) & (row % slots < counts)
        return jnp.where(keep, 1.0, 0.0).astype(jnp.bfloat16)

    near = jnp.minimum(place, line - 1 - place)
    far = jnp.maximum(place, line - 1 - place)

    def step_body(step, _):
        first_use = step - SKEW * near
        sub_now = first_use // rounds

        @pl.when((first_use >= 0) & (first_use < chunks) & (lax.rem(first_use + rounds, rounds) == 0))
        def _():
            own_copy(sub_now).wait()
            pair_arrival(sub_now).wait_recv()

            @pl.when(sub_now + 1 < subs)
            def _():
                pair_copy(sub_now + 1).start()

            for i in range(2):
                @pl.when(sub_now == i)
                def _():
                    bank_pair(i).start()

        k_right = step - SKEW * place

        @pl.when((k_right >= 0) & (k_right < chunks))
        def _():
            @pl.when(place > 0)
            def _():
                right_copy(k_right).wait_recv()

            @pl.when(place < line - 1)
            def _():
                out_right[k_right] = pick(k_right, in_left[k_right])
                right_copy(k_right).start()

        k_left = step - SKEW * (line - 1 - place)

        @pl.when((k_left >= 0) & (k_left < chunks))
        def _():
            @pl.when(place < line - 1)
            def _():
                left_copy(k_left).wait_recv()

            @pl.when(place > 0)
            def _():
                out_left[k_left] = pick(k_left, in_right[k_left])
                left_copy(k_left).start()

        k = step - SKEW * far

        @pl.when(k == 0)
        def _():
            bank_own.wait()
            bank_twin.wait_recv()

            def arrive(j, _):
                count_arrival(lax.rem(me + j, n)).wait_recv()
                return 0

            lax.fori_loop(1, n, arrive, 0)

        for i in range(2):
            @pl.when(k == BANK_LAG - 2 + i)
            def _():
                bank_pair(i).wait_recv()
                bank_relay(i).start()

        @pl.when(k == BANK_LAG)
        def _():
            for i in range(2):
                bank_relayed(i).wait_recv()

        @pl.when((k >= 0) & (k < chunks))
        def _():
            travelled = jnp.where(
                owner_place(k) < place,
                in_left[k].astype(jnp.float32),
                in_right[k].astype(jnp.float32),
            )
            query[k] = pick(k, travelled).T
            masks[k] = mask(k)
            score(k, 0)

        k_late = k - BANK_LAG

        @pl.when((k_late >= 0) & (k_late < chunks))
        def _():
            score(k_late, 1)

        return 0

    lax.fori_loop(0, chunks + SKEW * (line - 1) + BANK_LAG, step_body, 0)

    sends = [
        remote(acc.at[0], acc_in.at[0], acc_send.at[0], acc_recv.at[0], twin_id),
        remote(acc.at[1], acc_in.at[1], acc_send.at[1], acc_recv.at[1], mate_id),
        remote(acc.at[1], acc_in.at[2], acc_send.at[2], acc_recv.at[2], cross_id),
    ]
    for send in sends:
        send.start()

    def sent(j, _):
        count_copy(lax.rem(me + j, n)).wait_send()
        return 0

    lax.fori_loop(1, n, sent, 0)
    for sub in range(subs):
        pair_copy(sub).wait_send()
    bank_twin.wait_send()
    for i in range(2):
        bank_pair(i).wait_send()
        bank_relay(i).wait_send()

    def drain(k, _):
        @pl.when(place < line - 1)
        def _():
            right_copy(k).wait_send()

        @pl.when(place > 0)
        def _():
            left_copy(k).wait_send()

        return 0

    lax.fori_loop(0, chunks, drain, 0)
    for send in sends:
        send.wait()
    width = acc.shape[3]
    for r in range(rounds):
        total = acc[0, r] + acc_in[0, r] + acc_in[1, r] + acc_in[2, r]
        counts = counts_all[owner_ref[r]].astype(jnp.float32)
        out_ref[:, r * width : (r + 1) * width] = total / counts


def per_device(captions, caption_lengths, video_bank, owner_order):
    n = lax.axis_size("vid")
    parts = 2 * lax.axis_size("tok")
    _, blocks, slots, depth = captions.shape
    videos, tokens, _ = video_bank.shape
    rounds = owner_order.shape[0]
    rows = CHUNK_ROWS
    subs = blocks * slots // parts // rows
    chunks = subs * rounds
    bf16, f32 = jnp.bfloat16, jnp.float32
    stream = pltpu.VMEM((chunks, rows, depth), bf16)
    dma = pltpu.SemaphoreType.DMA
    logits = rounds * (blocks * slots // parts) * 2 * videos * 2 * tokens
    return pl.pallas_call(
        functools.partial(kernel, n, rounds, slots),
        out_shape=jax.ShapeDtypeStruct((videos, rounds * blocks), f32),
        in_specs=[
            pl.BlockSpec(memory_space=pltpu.HBM),
            pl.BlockSpec(memory_space=pltpu.VMEM),
            pl.BlockSpec(memory_space=pltpu.HBM),
            pl.BlockSpec(memory_space=pltpu.SMEM),
        ],
        out_specs=pl.BlockSpec(memory_space=pltpu.VMEM),
        scratch_shapes=[
            pltpu.VMEM((2, subs, rows, depth), bf16),
            stream, stream, stream, stream,
            pltpu.VMEM((chunks, depth, rows), bf16),
            pltpu.VMEM((2, videos, 2, tokens, depth), bf16),
            pltpu.VMEM((n, 1, blocks), jnp.int32),
            pltpu.VMEM((videos, 16, rows), f32),
            pltpu.VMEM((videos, 16, rows), f32),
            pltpu.VMEM((chunks, rows, blocks), bf16),
            pltpu.VMEM((2, rounds, videos, blocks), f32),
            pltpu.VMEM((3, rounds, videos, blocks), f32),
            dma((subs,)), dma, dma((subs,)), dma((subs,)),
            dma((chunks,)), dma((chunks,)), dma((chunks,)), dma((chunks,)),
            dma((n,)), dma((n,)), dma((5,)), dma((5,)), dma((3,)), dma((3,)),
        ],
        compiler_params=pltpu.CompilerParams(
            collective_id=0, has_side_effects=True, vmem_limit_bytes=64 * 1024 * 1024 - 256 * 1024
        ),
        cost_estimate=pl.CostEstimate(
            flops=2 * depth * logits, bytes_accessed=8 * 1024 * 1024, transcendentals=logits
        ),
    )(captions.reshape(blocks * slots, depth), caption_lengths, video_bank, owner_order)


def solution(mesh):
    return jax.shard_map(
        per_device,
        mesh=mesh,
        in_specs=(
            P(("groups", "vid"), None, None, None),
            P(("groups", "vid"), None),
            P(("groups", "vid"), "tok", None),
            P("groups"),
        ),
        out_specs=P(("groups", "vid"), None),
        check_vma=False,
    )
```

```python
import functools
import math

import jax
import jax.numpy as jnp
from jax import lax
from jax.experimental import pallas as pl
from jax.experimental.pallas import tpu as pltpu
from jax.sharding import PartitionSpec as P

sharpness_factor = 5.0
SCALE = sharpness_factor * math.log2(math.e)
UNSCALE = math.log(2.0) / sharpness_factor

CHUNK_ROWS = 256
LANES = 128
SKEW = 2
PIECES = 2
BANK_LAG = 4
MESH = pl.DeviceIdType.MESH


def kernel(
    n, rounds, slots,
    caps_ref, counts_ref, bank_ref, owner_ref, out_ref,
    mine, in_left, in_right, out_left, out_right, query, bank, counts_all, peaks, sums, masks, acc, acc_in,
    own_sem, bank_sem, pair_send, pair_recv, right_send, right_recv, left_send, left_recv,
    count_send, count_recv, bank_send, bank_recv, acc_send, acc_recv,
):
    me = lax.axis_index("vid")
    tok = lax.axis_index("tok")
    place = me // 2
    side = me % 2
    mate = me + 1 - 2 * side
    other = 1 - tok
    line = n // 2
    subs = mine.shape[1]
    rows = mine.shape[2]
    chunks = subs * rounds
    videos = bank.shape[1]
    half = videos // 2
    mate_id = {"vid": mate, "tok": tok}
    twin_id = {"vid": me, "tok": other}
    cross_id = {"vid": mate, "tok": other}
    right_id = {"vid": me + 2, "tok": tok}
    left_id = {"vid": me - 2, "tok": tok}

    def remote(src, dst, send, recv, device):
        return pltpu.make_async_remote_copy(
            src_ref=src, dst_ref=dst, send_sem=send, recv_sem=recv,
            device_id=device, device_id_type=MESH,
        )

    def block_rows(of_side, sub):
        quarter = of_side * 2 + tok
        return pl.ds(pl.multiple_of((quarter * subs + sub) * rows, rows), rows)

    def own_copy(sub):
        return pltpu.make_async_copy(
            caps_ref.at[block_rows(side, sub)], mine.at[side, sub], own_sem.at[sub]
        )

    def pair_copy(sub):
        return remote(
            caps_ref.at[block_rows(1 - side, sub)], mine.at[side, sub],
            pair_send.at[sub], pair_recv.at[sub], mate_id,
        )

    def pair_arrival(sub):
        return remote(
            mine.at[1 - side, sub], mine.at[1 - side, sub],
            pair_send.at[sub], pair_recv.at[sub], mate_id,
        )

    def part(i):
        return pl.ds(i * half, half)

    bank_own = pltpu.make_async_copy(bank_ref, bank.at[0, :, tok], bank_sem)
    bank_twin = remote(
        bank_ref, bank.at[0, :, tok], bank_send.at[0], bank_recv.at[0], twin_id
    )

    def bank_pair(i):
        return remote(
            bank_ref.at[part(i)], bank.at[1, part(i), tok],
            bank_send.at[1 + i], bank_recv.at[1 + i], mate_id,
        )

    def bank_relay(i):
        return remote(
            bank.at[1, part(i), tok], bank.at[1, part(i), tok],
            bank_send.at[3 + i], bank_recv.at[3 + i], twin_id,
        )

    def bank_relayed(i):
        return remote(
            bank.at[1, part(i), other], bank.at[1, part(i), other],
            bank_send.at[3 + i], bank_recv.at[3 + i], twin_id,
        )

    def piece(h):
        size = rows // PIECES
        return pl.ds(h * size, size)

    def right_copy(k, h):
        return remote(
            out_right.at[k, piece(h)], in_left.at[k, piece(h)],
            right_send.at[k, h], right_recv.at[k, h], right_id,
        )

    def left_copy(k, h):
        return remote(
            out_left.at[k, piece(h)], in_right.at[k, piece(h)],
            left_send.at[k, h], left_recv.at[k, h], left_id,
        )

    def count_copy(to):
        return remote(
            counts_all.at[me], counts_all.at[me], count_send.at[to], count_recv.at[me],
            {"vid": to, "tok": tok},
        )

    def count_arrival(source):
        return remote(
            counts_all.at[source], counts_all.at[source], count_send.at[source],
            count_recv.at[source], {"vid": source, "tok": tok},
        )

    barrier = pltpu.get_barrier_semaphore()

    def greet(j, _):
        to = lax.rem(me + j, n)
        pl.semaphore_signal(barrier, inc=1, device_id={"vid": to, "tok": tok}, device_id_type=MESH)
        return 0

    lax.fori_loop(1, n, greet, 0)
    for device in (twin_id, cross_id):
        pl.semaphore_signal(barrier, inc=1, device_id=device, device_id_type=MESH)
    for sub in range(subs):
        own_copy(sub).start()
    bank_own.start()
    counts_all[me] = counts_ref[...]
    acc[...] = jnp.zeros_like(acc)
    pl.semaphore_wait(barrier, n + 1)

    pair_copy(0).start()

    def push(j, _):
        count_copy(lax.rem(me + j, n)).start()
        return 0

    lax.fori_loop(1, n, push, 0)
    bank_twin.start()

    def owner_of(k):
        return owner_ref[lax.rem(k, rounds)]

    def candidate(k, span):
        sub = k // rounds
        first = mine[0, sub, span].astype(jnp.float32)
        second = mine[1, sub, span].astype(jnp.float32)
        owner_side = jnp.full(first.shape, lax.rem(owner_of(k), 2), jnp.int32)
        return jnp.where(owner_side == 0, first, second)

    def pick(k, incoming, span):
        owner_place = jnp.full(incoming.shape, owner_of(k) // 2, jnp.int32)
        return jnp.where(
            owner_place == place, candidate(k, span), incoming.astype(jnp.float32)
        ).astype(jnp.bfloat16)

    def score(k, slot):
        q = query[k]
        tiles = bank.shape[2]

        group = math.gcd(videos, 4)

        def similarity(g):
            tokens = bank[slot, g * group : (g + 1) * group]
            tokens = tokens.reshape(group * tiles * bank.shape[3], bank.shape[4])
            s = jnp.dot(tokens, q, preferred_element_type=jnp.float32)
            return s.reshape(group * tiles, bank.shape[3] // 8, 8, rows)

        ahead = similarity(0)
        for g in range(videos // group):
            now = ahead
            if (g + 1) * group < videos:
                ahead = similarity(g + 1)
            for b in range(group * tiles):
                for lane in range(0, rows, LANES):
                    block = now[b, :, :, lane : lane + LANES]
                    top = jnp.max(block, axis=0)
                    powers = jnp.exp2((block - top[None]) * SCALE)
                    video, tile = divmod(g * group * tiles + b, tiles)
                    peaks[video, tile * 8 : tile * 8 + 8, lane : lane + LANES] = top
                    sums[video, tile * 8 : tile * 8 + 8, lane : lane + LANES] = jnp.sum(powers, axis=0)
        tops = peaks[...]
        peak = jnp.max(tops, axis=1)
        weighed = sums[...] * jnp.exp2((tops - peak[:, None, :]) * SCALE)
        values = peak + UNSCALE * jnp.log2(jnp.sum(weighed, axis=1))
        r = lax.rem(k, rounds)
        keep = masks[k]
        high = values.astype(jnp.bfloat16)
        low = (values - high.astype(jnp.float32)).astype(jnp.bfloat16)
        acc[slot, r] += jnp.dot(high, keep, preferred_element_type=jnp.float32) + jnp.dot(
            low, keep, preferred_element_type=jnp.float32
        )

    def mask(k):
        first = ((side * 2 + tok) * subs + k // rounds) * (rows // slots)
        width = acc.shape[3]
        row = lax.broadcasted_iota(jnp.int32, (rows, width), 0)
        column = lax.broadcasted_iota(jnp.int32, (rows, width), 1)
        counts = counts_all[owner_of(k)]
        keep = (column == first + row // slots) & (row % slots < counts)
        return jnp.where(keep, 1.0, 0.0).astype(jnp.bfloat16)

    near = jnp.minimum(place, line - 1 - place)
    far = jnp.maximum(place, line - 1 - place)

    def step_body(step, _):
        first_use = step - SKEW * near
        sub_now = first_use // rounds

        @pl.when((first_use >= 0) & (first_use < chunks) & (lax.rem(first_use + rounds, rounds) == 0))
        def _():
            own_copy(sub_now).wait()
            pair_arrival(sub_now).wait_recv()

            @pl.when(sub_now + 1 < subs)
            def _():
                pair_copy(sub_now + 1).start()

            for i in range(2):
                @pl.when(sub_now == i)
                def _():
                    bank_pair(i).start()

        k_right = step - SKEW * place

        @pl.when((k_right >= 0) & (k_right < chunks))
        def _():
            for h in range(PIECES):
                @pl.when(place > 0)
                def _():
                    right_copy(k_right, h).wait_recv()

                @pl.when(place < line - 1)
                def _():
                    out_right[k_right, piece(h)] = pick(
                        k_right, in_left[k_right, piece(h)], piece(h)
                    )

                    @pl.when(k_right > 0)
                    def _():
                        right_copy(k_right - 1, h).wait_send()

                    right_copy(k_right, h).start()

        k_left = step - SKEW * (line - 1 - place)

        @pl.when((k_left >= 0) & (k_left < chunks))
        def _():
            for h in range(PIECES):
                @pl.when(place < line - 1)
                def _():
                    left_copy(k_left, h).wait_recv()

                @pl.when(place > 0)
                def _():
                    out_left[k_left, piece(h)] = pick(
                        k_left, in_right[k_left, piece(h)], piece(h)
                    )

                    @pl.when(k_left > 0)
                    def _():
                        left_copy(k_left - 1, h).wait_send()

                    left_copy(k_left, h).start()

        k = step - SKEW * far

        @pl.when(k == 0)
        def _():
            bank_own.wait()
            bank_twin.wait_recv()

            def arrive(j, _):
                count_arrival(lax.rem(me + j, n)).wait_recv()
                return 0

            lax.fori_loop(1, n, arrive, 0)

        for i in range(2):
            @pl.when(k == BANK_LAG - 2 + i)
            def _():
                bank_pair(i).wait_recv()
                bank_relay(i).start()

        @pl.when(k == BANK_LAG)
        def _():
            for i in range(2):
                bank_relayed(i).wait_recv()

        @pl.when((k >= 0) & (k < chunks))
        def _():
            travelled = jnp.where(
                jnp.full(in_left.shape[1:], owner_of(k) // 2, jnp.int32) < place,
                in_left[k].astype(jnp.float32),
                in_right[k].astype(jnp.float32),
            )
            query[k] = pick(k, travelled, pl.ds(0, rows)).T
            masks[k] = mask(k)
            score(k, 0)

        k_late = k - BANK_LAG

        @pl.when((k_late >= 0) & (k_late < chunks))
        def _():
            score(k_late, 1)

        return 0

    lax.fori_loop(0, chunks + SKEW * (line - 1) + BANK_LAG, step_body, 0)

    sends = [
        remote(acc.at[0], acc_in.at[0], acc_send.at[0], acc_recv.at[0], twin_id),
        remote(acc.at[1], acc_in.at[1], acc_send.at[1], acc_recv.at[1], mate_id),
        remote(acc.at[1], acc_in.at[2], acc_send.at[2], acc_recv.at[2], cross_id),
    ]
    for send in sends:
        send.start()

    def sent(j, _):
        count_copy(lax.rem(me + j, n)).wait_send()
        return 0

    lax.fori_loop(1, n, sent, 0)
    for sub in range(subs):
        pair_copy(sub).wait_send()
    bank_twin.wait_send()
    for i in range(2):
        bank_pair(i).wait_send()
        bank_relay(i).wait_send()

    for h in range(PIECES):
        @pl.when(place < line - 1)
        def _():
            right_copy(chunks - 1, h).wait_send()

        @pl.when(place > 0)
        def _():
            left_copy(chunks - 1, h).wait_send()

    for send in sends:
        send.wait()
    width = acc.shape[3]
    for r in range(rounds):
        total = acc[0, r] + acc_in[0, r] + acc_in[1, r] + acc_in[2, r]
        counts = counts_all[owner_ref[r]].astype(jnp.float32)
        out_ref[:, r * width : (r + 1) * width] = total / counts


def per_device(captions, caption_lengths, video_bank, owner_order):
    n = lax.axis_size("vid")
    parts = 2 * lax.axis_size("tok")
    _, blocks, slots, depth = captions.shape
    videos, tokens, _ = video_bank.shape
    rounds = owner_order.shape[0]
    rows = CHUNK_ROWS
    subs = blocks * slots // parts // rows
    chunks = subs * rounds
    bf16, f32 = jnp.bfloat16, jnp.float32
    stream = pltpu.VMEM((chunks, rows, depth), bf16)
    dma = pltpu.SemaphoreType.DMA
    logits = rounds * (blocks * slots // parts) * 2 * videos * 2 * tokens
    return pl.pallas_call(
        functools.partial(kernel, n, rounds, slots),
        out_shape=jax.ShapeDtypeStruct((videos, rounds * blocks), f32),
        in_specs=[
            pl.BlockSpec(memory_space=pltpu.HBM),
            pl.BlockSpec(memory_space=pltpu.VMEM),
            pl.BlockSpec(memory_space=pltpu.HBM),
            pl.BlockSpec(memory_space=pltpu.SMEM),
        ],
        out_specs=pl.BlockSpec(memory_space=pltpu.VMEM),
        scratch_shapes=[
            pltpu.VMEM((2, subs, rows, depth), bf16),
            stream, stream, stream, stream,
            pltpu.VMEM((chunks, depth, rows), bf16),
            pltpu.VMEM((2, videos, 2, tokens, depth), bf16),
            pltpu.VMEM((n, 1, blocks), jnp.int32),
            pltpu.VMEM((videos, 16, rows), f32),
            pltpu.VMEM((videos, 16, rows), f32),
            pltpu.VMEM((chunks, rows, blocks), bf16),
            pltpu.VMEM((2, rounds, videos, blocks), f32),
            pltpu.VMEM((3, rounds, videos, blocks), f32),
            dma((subs,)), dma, dma((subs,)), dma((subs,)),
            dma((chunks, PIECES)), dma((chunks, PIECES)),
            dma((chunks, PIECES)), dma((chunks, PIECES)),
            dma((n,)), dma((n,)), dma((5,)), dma((5,)), dma((3,)), dma((3,)),
        ],
        compiler_params=pltpu.CompilerParams(
            collective_id=0, has_side_effects=True, vmem_limit_bytes=64 * 1024 * 1024 - 256 * 1024
        ),
        cost_estimate=pl.CostEstimate(
            flops=2 * depth * logits, bytes_accessed=8 * 1024 * 1024, transcendentals=logits
        ),
    )(captions.reshape(blocks * slots, depth), caption_lengths, video_bank, owner_order)


def solution(mesh):
    return jax.shard_map(
        per_device,
        mesh=mesh,
        in_specs=(
            P(("groups", "vid"), None, None, None),
            P(("groups", "vid"), None),
            P(("groups", "vid"), "tok", None),
            P("groups"),
        ),
        out_specs=P(("groups", "vid"), None),
        check_vma=False,
    )
```

```python
import functools
import math

import jax
import jax.numpy as jnp
from jax import lax
from jax.experimental import pallas as pl
from jax.experimental.pallas import tpu as pltpu
from jax.sharding import PartitionSpec as P

sharpness_factor = 5.0
SCALE = sharpness_factor * math.log2(math.e)
UNSCALE = math.log(2.0) / sharpness_factor

CHUNK_ROWS = 256
LANES = 128
SKEW = 3
BANK_LAG = 4
MESH = pl.DeviceIdType.MESH


def kernel(
    n, rounds, slots,
    caps_ref, counts_ref, bank_ref, owner_ref, out_ref,
    mine, in_left, in_right, out_left, out_right, query, bank, counts_all, peaks, sums, masks, acc, acc_in,
    own_sem, bank_sem, pair_send, pair_recv, right_send, right_recv, left_send, left_recv,
    count_send, count_recv, bank_send, bank_recv, acc_send, acc_recv,
):
    me = lax.axis_index("vid")
    tok = lax.axis_index("tok")
    place = me // 2
    side = me % 2
    mate = me + 1 - 2 * side
    other = 1 - tok
    line = n // 2
    subs = mine.shape[1]
    rows = mine.shape[2]
    chunks = subs * rounds
    videos = bank.shape[1]
    half = videos // 2
    mate_id = {"vid": mate, "tok": tok}
    twin_id = {"vid": me, "tok": other}
    cross_id = {"vid": mate, "tok": other}
    right_id = {"vid": me + 2, "tok": tok}
    left_id = {"vid": me - 2, "tok": tok}

    def remote(src, dst, send, recv, device):
        return pltpu.make_async_remote_copy(
            src_ref=src, dst_ref=dst, send_sem=send, recv_sem=recv,
            device_id=device, device_id_type=MESH,
        )

    def block_rows(of_side, sub):
        quarter = of_side * 2 + tok
        return pl.ds(pl.multiple_of((quarter * subs + sub) * rows, rows), rows)

    def own_copy(sub):
        return pltpu.make_async_copy(
            caps_ref.at[block_rows(side, sub)], mine.at[side, sub], own_sem.at[sub]
        )

    def pair_copy(sub):
        return remote(
            caps_ref.at[block_rows(1 - side, sub)], mine.at[side, sub],
            pair_send.at[sub], pair_recv.at[sub], mate_id,
        )

    def pair_arrival(sub):
        return remote(
            mine.at[1 - side, sub], mine.at[1 - side, sub],
            pair_send.at[sub], pair_recv.at[sub], mate_id,
        )

    def part(i):
        return pl.ds(i * half, half)

    bank_own = pltpu.make_async_copy(bank_ref, bank.at[0, :, tok], bank_sem)
    bank_twin = remote(
        bank_ref, bank.at[0, :, tok], bank_send.at[0], bank_recv.at[0], twin_id
    )

    def bank_pair(i):
        return remote(
            bank_ref.at[part(i)], bank.at[1, part(i), tok],
            bank_send.at[1 + i], bank_recv.at[1 + i], mate_id,
        )

    def bank_relay(i):
        return remote(
            bank.at[1, part(i), tok], bank.at[1, part(i), tok],
            bank_send.at[3 + i], bank_recv.at[3 + i], twin_id,
        )

    def bank_relayed(i):
        return remote(
            bank.at[1, part(i), other], bank.at[1, part(i), other],
            bank_send.at[3 + i], bank_recv.at[3 + i], twin_id,
        )

    def right_copy(k):
        return remote(
            out_right.at[k], in_left.at[k], right_send.at[k], right_recv.at[k], right_id
        )

    def left_copy(k):
        return remote(
            out_left.at[k], in_right.at[k], left_send.at[k], left_recv.at[k], left_id
        )

    def count_copy(to):
        return remote(
            counts_all.at[me], counts_all.at[me], count_send.at[to], count_recv.at[me],
            {"vid": to, "tok": tok},
        )

    def count_arrival(source):
        return remote(
            counts_all.at[source], counts_all.at[source], count_send.at[source],
            count_recv.at[source], {"vid": source, "tok": tok},
        )

    barrier = pltpu.get_barrier_semaphore()

    def greet(j, _):
        to = lax.rem(me + j, n)
        pl.semaphore_signal(barrier, inc=1, device_id={"vid": to, "tok": tok}, device_id_type=MESH)
        return 0

    lax.fori_loop(1, n, greet, 0)
    for device in (twin_id, cross_id):
        pl.semaphore_signal(barrier, inc=1, device_id=device, device_id_type=MESH)
    for sub in range(subs):
        own_copy(sub).start()
    bank_own.start()
    counts_all[me] = counts_ref[...]
    acc[...] = jnp.zeros_like(acc)
    pl.semaphore_wait(barrier, n + 1)

    pair_copy(0).start()

    def push(j, _):
        count_copy(lax.rem(me + j, n)).start()
        return 0

    lax.fori_loop(1, n, push, 0)
    bank_twin.start()

    def owner_of(k):
        return owner_ref[lax.rem(k, rounds)]

    def candidate(k):
        sub = k // rounds
        owner_side = jnp.full((rows, mine.shape[3]), lax.rem(owner_of(k), 2), jnp.int32)
        return jnp.where(
            owner_side == 0,
            mine[0, sub].astype(jnp.float32),
            mine[1, sub].astype(jnp.float32),
        )

    def owner_place(k):
        return jnp.full((rows, mine.shape[3]), owner_of(k) // 2, jnp.int32)

    def pick(k, incoming):
        return jnp.where(
            owner_place(k) == place, candidate(k), incoming.astype(jnp.float32)
        ).astype(jnp.bfloat16)

    def score(k, slot):
        q = query[k]
        tiles = bank.shape[2]

        group = math.gcd(videos, 4)

        def similarity(g):
            tokens = bank[slot, g * group : (g + 1) * group]
            tokens = tokens.reshape(group * tiles * bank.shape[3], bank.shape[4])
            tokens = jnp.concatenate([tokens, tokens], axis=1)
            s = jnp.dot(tokens, q, preferred_element_type=jnp.float32)
            return s.reshape(group * tiles, bank.shape[3] // 8, 8, rows)

        ahead = similarity(0)
        for g in range(videos // group):
            now = ahead
            if (g + 1) * group < videos:
                ahead = similarity(g + 1)
            for b in range(group * tiles):
                for lane in range(0, rows, LANES):
                    block = now[b, :, :, lane : lane + LANES]
                    top = jnp.max(block, axis=0)
                    powers = jnp.exp2(block - top[None])
                    video, tile = divmod(g * group * tiles + b, tiles)
                    peaks[video, tile * 8 : tile * 8 + 8, lane : lane + LANES] = top
                    sums[video, tile * 8 : tile * 8 + 8, lane : lane + LANES] = jnp.sum(powers, axis=0)
        tops = peaks[...]
        peak = jnp.max(tops, axis=1)
        weighed = sums[...] * jnp.exp2(tops - peak[:, None, :])
        values = UNSCALE * (peak + jnp.log2(jnp.sum(weighed, axis=1)))
        r = lax.rem(k, rounds)
        keep = masks[k]
        high = values.astype(jnp.bfloat16)
        low = (values - high.astype(jnp.float32)).astype(jnp.bfloat16)
        acc[slot, r] += jnp.dot(high, keep, preferred_element_type=jnp.float32) + jnp.dot(
            low, keep, preferred_element_type=jnp.float32
        )

    def mask(k):
        first = ((side * 2 + tok) * subs + k // rounds) * (rows // slots)
        width = acc.shape[3]
        row = lax.broadcasted_iota(jnp.int32, (rows, width), 0)
        column = lax.broadcasted_iota(jnp.int32, (rows, width), 1)
        counts = counts_all[owner_of(k)]
        keep = (column == first + row // slots) & (row % slots < counts)
        return jnp.where(keep, 1.0, 0.0).astype(jnp.bfloat16)

    near = jnp.minimum(place, line - 1 - place)
    far = jnp.maximum(place, line - 1 - place)

    def step_body(step, _):
        first_use = step - SKEW * near
        sub_now = first_use // rounds

        @pl.when((first_use >= 0) & (first_use < chunks) & (lax.rem(first_use + rounds, rounds) == 0))
        def _():
            own_copy(sub_now).wait()
            pair_arrival(sub_now).wait_recv()

            @pl.when(sub_now + 1 < subs)
            def _():
                pair_copy(sub_now + 1).start()

            for i in range(2):
                @pl.when(sub_now == i)
                def _():
                    bank_pair(i).start()

        k_right = step - SKEW * place

        @pl.when((k_right >= 0) & (k_right < chunks))
        def _():
            @pl.when(place > 0)
            def _():
                right_copy(k_right).wait_recv()

            @pl.when(place < line - 1)
            def _():
                out_right[k_right] = pick(k_right, in_left[k_right])
                right_copy(k_right).start()

        k_left = step - SKEW * (line - 1 - place)

        @pl.when((k_left >= 0) & (k_left < chunks))
        def _():
            @pl.when(place < line - 1)
            def _():
                left_copy(k_left).wait_recv()

            @pl.when(place > 0)
            def _():
                out_left[k_left] = pick(k_left, in_right[k_left])
                left_copy(k_left).start()

        k = step - SKEW * far

        @pl.when(k == 0)
        def _():
            bank_own.wait()
            bank_twin.wait_recv()

            def arrive(j, _):
                count_arrival(lax.rem(me + j, n)).wait_recv()
                return 0

            lax.fori_loop(1, n, arrive, 0)

        for i in range(2):
            @pl.when(k == BANK_LAG - 2 + i)
            def _():
                bank_pair(i).wait_recv()
                bank_relay(i).start()

        @pl.when(k == BANK_LAG)
        def _():
            for i in range(2):
                bank_relayed(i).wait_recv()

        @pl.when((k >= 0) & (k < chunks))
        def _():
            travelled = jnp.where(
                owner_place(k) < place,
                in_left[k].astype(jnp.float32),
                in_right[k].astype(jnp.float32),
            )
            scaled = pick(k, travelled).astype(jnp.float32) * SCALE
            upper = scaled.astype(jnp.bfloat16)
            lower = (scaled - upper.astype(jnp.float32)).astype(jnp.bfloat16)
            query[k] = jnp.concatenate([upper.T, lower.T], axis=0)
            masks[k] = mask(k)
            score(k, 0)

        k_late = k - BANK_LAG

        @pl.when((k_late >= 0) & (k_late < chunks))
        def _():
            score(k_late, 1)

        return 0

    lax.fori_loop(0, chunks + SKEW * (line - 1) + BANK_LAG, step_body, 0)

    sends = [
        remote(acc.at[0], acc_in.at[0], acc_send.at[0], acc_recv.at[0], twin_id),
        remote(acc.at[1], acc_in.at[1], acc_send.at[1], acc_recv.at[1], mate_id),
        remote(acc.at[1], acc_in.at[2], acc_send.at[2], acc_recv.at[2], cross_id),
    ]
    for send in sends:
        send.start()

    def sent(j, _):
        count_copy(lax.rem(me + j, n)).wait_send()
        return 0

    lax.fori_loop(1, n, sent, 0)
    for sub in range(subs):
        pair_copy(sub).wait_send()
    bank_twin.wait_send()
    for i in range(2):
        bank_pair(i).wait_send()
        bank_relay(i).wait_send()

    def drain(k, _):
        @pl.when(place < line - 1)
        def _():
            right_copy(k).wait_send()

        @pl.when(place > 0)
        def _():
            left_copy(k).wait_send()

        return 0

    lax.fori_loop(0, chunks, drain, 0)
    for send in sends:
        send.wait()
    width = acc.shape[3]
    for r in range(rounds):
        total = acc[0, r] + acc_in[0, r] + acc_in[1, r] + acc_in[2, r]
        counts = counts_all[owner_ref[r]].astype(jnp.float32)
        out_ref[:, r * width : (r + 1) * width] = total / counts


def per_device(captions, caption_lengths, video_bank, owner_order):
    n = lax.axis_size("vid")
    parts = 2 * lax.axis_size("tok")
    _, blocks, slots, depth = captions.shape
    videos, tokens, _ = video_bank.shape
    rounds = owner_order.shape[0]
    rows = CHUNK_ROWS
    subs = blocks * slots // parts // rows
    chunks = subs * rounds
    bf16, f32 = jnp.bfloat16, jnp.float32
    stream = pltpu.VMEM((chunks, rows, depth), bf16)
    dma = pltpu.SemaphoreType.DMA
    logits = rounds * (blocks * slots // parts) * 2 * videos * 2 * tokens
    return pl.pallas_call(
        functools.partial(kernel, n, rounds, slots),
        out_shape=jax.ShapeDtypeStruct((videos, rounds * blocks), f32),
        in_specs=[
            pl.BlockSpec(memory_space=pltpu.HBM),
            pl.BlockSpec(memory_space=pltpu.VMEM),
            pl.BlockSpec(memory_space=pltpu.HBM),
            pl.BlockSpec(memory_space=pltpu.SMEM),
        ],
        out_specs=pl.BlockSpec(memory_space=pltpu.VMEM),
        scratch_shapes=[
            pltpu.VMEM((2, subs, rows, depth), bf16),
            stream, stream, stream, stream,
            pltpu.VMEM((chunks, 2 * depth, rows), bf16),
            pltpu.VMEM((2, videos, 2, tokens, depth), bf16),
            pltpu.VMEM((n, 1, blocks), jnp.int32),
            pltpu.VMEM((videos, 16, rows), f32),
            pltpu.VMEM((videos, 16, rows), f32),
            pltpu.VMEM((chunks, rows, blocks), bf16),
            pltpu.VMEM((2, rounds, videos, blocks), f32),
            pltpu.VMEM((3, rounds, videos, blocks), f32),
            dma((subs,)), dma, dma((subs,)), dma((subs,)),
            dma((chunks,)), dma((chunks,)), dma((chunks,)), dma((chunks,)),
            dma((n,)), dma((n,)), dma((5,)), dma((5,)), dma((3,)), dma((3,)),
        ],
        compiler_params=pltpu.CompilerParams(
            collective_id=0, has_side_effects=True, vmem_limit_bytes=64 * 1024 * 1024 - 256 * 1024
        ),
        cost_estimate=pl.CostEstimate(
            flops=2 * depth * logits, bytes_accessed=8 * 1024 * 1024, transcendentals=logits
        ),
    )(captions.reshape(blocks * slots, depth), caption_lengths, video_bank, owner_order)


def solution(mesh):
    return jax.shard_map(
        per_device,
        mesh=mesh,
        in_specs=(
            P(("groups", "vid"), None, None, None),
            P(("groups", "vid"), None),
            P(("groups", "vid"), "tok", None),
            P("groups"),
        ),
        out_specs=P(("groups", "vid"), None),
        check_vma=False,
    )
```

```python
import functools
import math

import jax
import jax.numpy as jnp
from jax import lax
from jax.experimental import pallas as pl
from jax.experimental.pallas import tpu as pltpu
from jax.sharding import PartitionSpec as P

sharpness_factor = 5.0
SCALE = sharpness_factor * math.log2(math.e)
UNSCALE = math.log(2.0) / sharpness_factor

CHUNK_ROWS = 256
LANES = 128
SKEW = 4
BANK_LAG = 4
MESH = pl.DeviceIdType.MESH


def kernel(
    n, rounds, slots,
    caps_ref, counts_ref, bank_ref, owner_ref, out_ref,
    mine, in_left, in_right, out_left, out_right, query, bank, counts_all, peaks, sums, masks, acc, acc_in,
    own_sem, bank_sem, pair_send, pair_recv, right_send, right_recv, left_send, left_recv,
    count_send, count_recv, bank_send, bank_recv, acc_send, acc_recv,
):
    me = lax.axis_index("vid")
    tok = lax.axis_index("tok")
    place = me // 2
    side = me % 2
    mate = me + 1 - 2 * side
    other = 1 - tok
    line = n // 2
    subs = mine.shape[1]
    rows = mine.shape[2]
    chunks = subs * rounds
    videos = bank.shape[1]
    half = videos // 2
    mate_id = {"vid": mate, "tok": tok}
    twin_id = {"vid": me, "tok": other}
    cross_id = {"vid": mate, "tok": other}
    right_id = {"vid": me + 2, "tok": tok}
    left_id = {"vid": me - 2, "tok": tok}

    def remote(src, dst, send, recv, device):
        return pltpu.make_async_remote_copy(
            src_ref=src, dst_ref=dst, send_sem=send, recv_sem=recv,
            device_id=device, device_id_type=MESH,
        )

    def block_rows(of_side, sub):
        quarter = of_side * 2 + tok
        return pl.ds(pl.multiple_of((quarter * subs + sub) * rows, rows), rows)

    def own_copy(sub):
        return pltpu.make_async_copy(
            caps_ref.at[block_rows(side, sub)], mine.at[side, sub], own_sem.at[sub]
        )

    def pair_copy(sub):
        return remote(
            caps_ref.at[block_rows(1 - side, sub)], mine.at[side, sub],
            pair_send.at[sub], pair_recv.at[sub], mate_id,
        )

    def pair_arrival(sub):
        return remote(
            mine.at[1 - side, sub], mine.at[1 - side, sub],
            pair_send.at[sub], pair_recv.at[sub], mate_id,
        )

    def part(i):
        return pl.ds(i * half, half)

    bank_own = pltpu.make_async_copy(bank_ref, bank.at[0, :, tok], bank_sem)
    bank_twin = remote(
        bank_ref, bank.at[0, :, tok], bank_send.at[0], bank_recv.at[0], twin_id
    )

    def bank_pair(i):
        return remote(
            bank_ref.at[part(i)], bank.at[1, part(i), tok],
            bank_send.at[1 + i], bank_recv.at[1 + i], mate_id,
        )

    def bank_relay(i):
        return remote(
            bank.at[1, part(i), tok], bank.at[1, part(i), tok],
            bank_send.at[3 + i], bank_recv.at[3 + i], twin_id,
        )

    def bank_relayed(i):
        return remote(
            bank.at[1, part(i), other], bank.at[1, part(i), other],
            bank_send.at[3 + i], bank_recv.at[3 + i], twin_id,
        )

    def right_copy(k):
        return remote(
            out_right.at[k], in_left.at[k], right_send.at[k], right_recv.at[k], right_id
        )

    def left_copy(k):
        return remote(
            out_left.at[k], in_right.at[k], left_send.at[k], left_recv.at[k], left_id
        )

    def count_copy(to):
        return remote(
            counts_all.at[me], counts_all.at[me], count_send.at[to], count_recv.at[me],
            {"vid": to, "tok": tok},
        )

    def count_arrival(source):
        return remote(
            counts_all.at[source], counts_all.at[source], count_send.at[source],
            count_recv.at[source], {"vid": source, "tok": tok},
        )

    barrier = pltpu.get_barrier_semaphore()

    def greet(j, _):
        to = lax.rem(me + j, n)
        pl.semaphore_signal(barrier, inc=1, device_id={"vid": to, "tok": tok}, device_id_type=MESH)
        return 0

    lax.fori_loop(1, n, greet, 0)
    for device in (twin_id, cross_id):
        pl.semaphore_signal(barrier, inc=1, device_id=device, device_id_type=MESH)
    for sub in range(subs):
        own_copy(sub).start()
    bank_own.start()
    counts_all[me] = counts_ref[...]
    acc[...] = jnp.zeros_like(acc)
    pl.semaphore_wait(barrier, n + 1)

    pair_copy(0).start()

    def push(j, _):
        count_copy(lax.rem(me + j, n)).start()
        return 0

    lax.fori_loop(1, n, push, 0)
    bank_twin.start()

    def owner_of(k):
        return owner_ref[lax.rem(k, rounds)]

    def candidate(k):
        sub = k // rounds
        owner_side = jnp.full((rows, mine.shape[3]), lax.rem(owner_of(k), 2), jnp.int32)
        return jnp.where(
            owner_side == 0,
            mine[0, sub].astype(jnp.float32),
            mine[1, sub].astype(jnp.float32),
        )

    def owner_place(k):
        return jnp.full((rows, mine.shape[3]), owner_of(k) // 2, jnp.int32)

    def pick(k, incoming):
        return jnp.where(
            owner_place(k) == place, candidate(k), incoming.astype(jnp.float32)
        ).astype(jnp.bfloat16)

    def score(k, slot):
        q = query[k]
        tiles = bank.shape[2]

        group = math.gcd(videos, 4)

        def similarity(g):
            tokens = bank[slot, g * group : (g + 1) * group]
            tokens = tokens.reshape(group * tiles * bank.shape[3], bank.shape[4])
            tokens = jnp.concatenate([tokens, tokens], axis=1)
            s = jnp.dot(tokens, q, preferred_element_type=jnp.float32)
            return s.reshape(group * tiles, bank.shape[3] // 8, 8, rows)

        ahead = similarity(0)
        for g in range(videos // group):
            now = ahead
            if (g + 1) * group < videos:
                ahead = similarity(g + 1)
            for b in range(group * tiles):
                for lane in range(0, rows, LANES):
                    block = now[b, :, :, lane : lane + LANES]
                    top = jnp.max(block, axis=0)
                    powers = jnp.exp2(block - top[None])
                    video, tile = divmod(g * group * tiles + b, tiles)
                    peaks[video, tile * 8 : tile * 8 + 8, lane : lane + LANES] = top
                    sums[video, tile * 8 : tile * 8 + 8, lane : lane + LANES] = jnp.sum(powers, axis=0)
        tops = peaks[...]
        peak = jnp.max(tops, axis=1)
        weighed = sums[...] * jnp.exp2(tops - peak[:, None, :])
        values = UNSCALE * (peak + jnp.log2(jnp.sum(weighed, axis=1)))
        r = lax.rem(k, rounds)
        keep = masks[k]
        high = values.astype(jnp.bfloat16)
        low = (values - high.astype(jnp.float32)).astype(jnp.bfloat16)
        acc[slot, r] += jnp.dot(high, keep, preferred_element_type=jnp.float32) + jnp.dot(
            low, keep, preferred_element_type=jnp.float32
        )

    def mask(k):
        first = ((side * 2 + tok) * subs + k // rounds) * (rows // slots)
        width = acc.shape[3]
        row = lax.broadcasted_iota(jnp.int32, (rows, width), 0)
        column = lax.broadcasted_iota(jnp.int32, (rows, width), 1)
        counts = counts_all[owner_of(k)]
        keep = (column == first + row // slots) & (row % slots < counts)
        return jnp.where(keep, 1.0, 0.0).astype(jnp.bfloat16)

    near = jnp.minimum(place, line - 1 - place)
    far = jnp.maximum(place, line - 1 - place)

    def step_body(step, _):
        first_use = step - SKEW * near
        sub_now = first_use // rounds

        @pl.when((first_use >= 0) & (first_use < chunks) & (lax.rem(first_use + rounds, rounds) == 0))
        def _():
            own_copy(sub_now).wait()
            pair_arrival(sub_now).wait_recv()

            @pl.when(sub_now + 1 < subs)
            def _():
                pair_copy(sub_now + 1).start()

            for i in range(2):
                @pl.when(sub_now == i)
                def _():
                    bank_pair(i).start()

        k_right = step - SKEW * place

        @pl.when((k_right >= 0) & (k_right < chunks))
        def _():
            @pl.when(place > 0)
            def _():
                right_copy(k_right).wait_recv()

            @pl.when(place < line - 1)
            def _():
                out_right[k_right] = pick(k_right, in_left[k_right])
                right_copy(k_right).start()

        k_left = step - SKEW * (line - 1 - place)

        @pl.when((k_left >= 0) & (k_left < chunks))
        def _():
            @pl.when(place < line - 1)
            def _():
                left_copy(k_left).wait_recv()

            @pl.when(place > 0)
            def _():
                out_left[k_left] = pick(k_left, in_right[k_left])
                left_copy(k_left).start()

        k = step - SKEW * far

        @pl.when(k == 0)
        def _():
            bank_own.wait()
            bank_twin.wait_recv()

            def arrive(j, _):
                count_arrival(lax.rem(me + j, n)).wait_recv()
                return 0

            lax.fori_loop(1, n, arrive, 0)

        for i in range(2):
            @pl.when(k == BANK_LAG - 2 + i)
            def _():
                bank_pair(i).wait_recv()
                bank_relay(i).start()

        @pl.when(k == BANK_LAG)
        def _():
            for i in range(2):
                bank_relayed(i).wait_recv()

        @pl.when((k >= 0) & (k < chunks))
        def _():
            travelled = jnp.where(
                owner_place(k) < place,
                in_left[k].astype(jnp.float32),
                in_right[k].astype(jnp.float32),
            )
            scaled = pick(k, travelled).astype(jnp.float32) * SCALE
            upper = scaled.astype(jnp.bfloat16)
            lower = (scaled - upper.astype(jnp.float32)).astype(jnp.bfloat16)
            query[k] = jnp.concatenate([upper.T, lower.T], axis=0)
            masks[k] = mask(k)
            score(k, 0)

        k_late = k - BANK_LAG

        @pl.when((k_late >= 0) & (k_late < chunks))
        def _():
            score(k_late, 1)

        return 0

    lax.fori_loop(0, chunks + SKEW * (line - 1) + BANK_LAG, step_body, 0)

    sends = [
        remote(acc.at[0], acc_in.at[0], acc_send.at[0], acc_recv.at[0], twin_id),
        remote(acc.at[1], acc_in.at[1], acc_send.at[1], acc_recv.at[1], mate_id),
        remote(acc.at[1], acc_in.at[2], acc_send.at[2], acc_recv.at[2], cross_id),
    ]
    for send in sends:
        send.start()

    def sent(j, _):
        count_copy(lax.rem(me + j, n)).wait_send()
        return 0

    lax.fori_loop(1, n, sent, 0)
    for sub in range(subs):
        pair_copy(sub).wait_send()
    bank_twin.wait_send()
    for i in range(2):
        bank_pair(i).wait_send()
        bank_relay(i).wait_send()

    def drain(k, _):
        @pl.when(place < line - 1)
        def _():
            right_copy(k).wait_send()

        @pl.when(place > 0)
        def _():
            left_copy(k).wait_send()

        return 0

    lax.fori_loop(0, chunks, drain, 0)
    for send in sends:
        send.wait()
    width = acc.shape[3]
    for r in range(rounds):
        total = acc[0, r] + acc_in[0, r] + acc_in[1, r] + acc_in[2, r]
        counts = counts_all[owner_ref[r]].astype(jnp.float32)
        out_ref[:, r * width : (r + 1) * width] = total / counts


def per_device(captions, caption_lengths, video_bank, owner_order):
    n = lax.axis_size("vid")
    parts = 2 * lax.axis_size("tok")
    _, blocks, slots, depth = captions.shape
    videos, tokens, _ = video_bank.shape
    rounds = owner_order.shape[0]
    rows = CHUNK_ROWS
    subs = blocks * slots // parts // rows
    chunks = subs * rounds
    bf16, f32 = jnp.bfloat16, jnp.float32
    stream = pltpu.VMEM((chunks, rows, depth), bf16)
    dma = pltpu.SemaphoreType.DMA
    logits = rounds * (blocks * slots // parts) * 2 * videos * 2 * tokens
    return pl.pallas_call(
        functools.partial(kernel, n, rounds, slots),
        out_shape=jax.ShapeDtypeStruct((videos, rounds * blocks), f32),
        in_specs=[
            pl.BlockSpec(memory_space=pltpu.HBM),
            pl.BlockSpec(memory_space=pltpu.VMEM),
            pl.BlockSpec(memory_space=pltpu.HBM),
            pl.BlockSpec(memory_space=pltpu.SMEM),
        ],
        out_specs=pl.BlockSpec(memory_space=pltpu.VMEM),
        scratch_shapes=[
            pltpu.VMEM((2, subs, rows, depth), bf16),
            stream, stream, stream, stream,
            pltpu.VMEM((chunks, 2 * depth, rows), bf16),
            pltpu.VMEM((2, videos, 2, tokens, depth), bf16),
            pltpu.VMEM((n, 1, blocks), jnp.int32),
            pltpu.VMEM((videos, 16, rows), f32),
            pltpu.VMEM((videos, 16, rows), f32),
            pltpu.VMEM((chunks, rows, blocks), bf16),
            pltpu.VMEM((2, rounds, videos, blocks), f32),
            pltpu.VMEM((3, rounds, videos, blocks), f32),
            dma((subs,)), dma, dma((subs,)), dma((subs,)),
            dma((chunks,)), dma((chunks,)), dma((chunks,)), dma((chunks,)),
            dma((n,)), dma((n,)), dma((5,)), dma((5,)), dma((3,)), dma((3,)),
        ],
        compiler_params=pltpu.CompilerParams(
            collective_id=0, has_side_effects=True, vmem_limit_bytes=64 * 1024 * 1024 - 256 * 1024
        ),
        cost_estimate=pl.CostEstimate(
            flops=2 * depth * logits, bytes_accessed=8 * 1024 * 1024, transcendentals=logits
        ),
    )(captions.reshape(blocks * slots, depth), caption_lengths, video_bank, owner_order)


def solution(mesh):
    return jax.shard_map(
        per_device,
        mesh=mesh,
        in_specs=(
            P(("groups", "vid"), None, None, None),
            P(("groups", "vid"), None),
            P(("groups", "vid"), "tok", None),
            P("groups"),
        ),
        out_specs=P(("groups", "vid"), None),
        check_vma=False,
    )
```
